32 devices in a mesh: grp: 2 (over core), mem: 16 (over z, y, x).
Axes of the slice: x: 2, y: 2, z: 4, core: 2. Of those that a mesh axis runs over, the one named last changes fastest.
Arguments:
- spectra: bfloat16 [256, 2, 16, 512], P(('grp', 'mem')), may hold values from -40 to 40
- partners: int32 [1, 16], replicated, may hold values from 0 to 1, as said below
Outputs:
- correlations: bfloat16 [256, 1, 128, 513], P(('grp', 'mem'))
The draws below stay inside these ranges and needn't reach their ends.
Inputs may be any that keep to these rules, and one draw needn't show every extreme that they name: For each member index k the offsets partners[r, k] of the rounds are distinct (offset 0 pairs a block with its own group).
All inputs are finite; a program needn't handle non-finite values.
Results may differ from the reference program's by a relative error of at most 0.0068.
Values may be sent and summed in bfloat16 or wider, within the bound.
A program may use at most 128 MiB of HBM per device.

```python
import math
import jax
import jax.numpy as jnp
from jax import lax

CH_DEV = 8
SEG = 16
BINS = 512
SMOOTH = 32
LAGS = 513
GRP_CH = 128
NCH = 256
R_WIN = 1
N_GRP = 2
N_MEM = 16


def draw_spectra(key, part):
    key_base = jax.random.fold_in(key, 11)
    key_level = jax.random.fold_in(key, 12)
    key_colour = jax.random.fold_in(key, 13)
    raw_values = jnp.clip(jax.random.normal(key_base, (NCH, 2, SEG, BINS), jnp.float32), -5.9, 5.9)
    loudness = jnp.exp(jax.random.uniform(key_level, (NCH, 1, SEG, 1), jnp.float32, -1.2, 1.2))
    colour = jnp.exp(jax.random.uniform(key_colour, (NCH, 1, 1, BINS), jnp.float32, -0.7, 0.7))
    return (raw_values * loudness * colour).astype(jnp.bfloat16)


def member_offsets(member_key):
    return jax.random.permutation(member_key, N_GRP)[:R_WIN].astype(jnp.int32)


def draw_partners(key, part):
    member_keys = jax.random.split(jax.random.fold_in(key, 21), N_MEM)
    table = jax.vmap(member_offsets)(member_keys)
    return jnp.transpose(table).astype(jnp.int32)


def setup_inputs(seed: int = 0) -> dict:
    key_list = jax.random.split(jax.random.key(seed), 3)
    spectra = draw_spectra(jax.random.fold_in(key_list[2], 71), 0)
    partners = draw_partners(jax.random.fold_in(key_list[2], 71), 0)
    return dict(spectra=spectra, partners=partners)


def whiten(spectra, half_width):
    components = spectra.astype(jnp.float32)
    power_sum = components[:, 0] * components[:, 0] + components[:, 1] * components[:, 1]
    bin_count = power_sum.shape[-1]
    positions = jnp.arange(bin_count, dtype=jnp.int32)
    band_matrix = (jnp.abs(positions[:, None] - positions[None, :]) <= half_width).astype(jnp.float32)
    smooth = jnp.dot(power_sum.reshape(-1, bin_count), band_matrix, precision=lax.Precision.HIGHEST)
    smooth = smooth.reshape(power_sum.shape) / (2 * half_width + 1)
    inv_level = lax.rsqrt(smooth + 1e-05)
    return (components * inv_level[:, None]).astype(jnp.bfloat16)

def lag_table(bin_count):
    centre = bin_count // 2
    frequency = jnp.arange(bin_count, dtype=jnp.int32)[:, None]
    lag_offset = jnp.arange(bin_count + 1, dtype=jnp.int32)[None, :] - centre
    angles = jnp.mod(frequency * lag_offset, 2 * bin_count).astype(jnp.float32) * (math.pi / bin_count)
    return jnp.stack([jnp.cos(angles), -jnp.sin(angles)], 0).astype(jnp.bfloat16)

def pair_lags(own_block, partner_block, transform):
    factor = math.sqrt(2.0 / (own_block.shape[3] * own_block.shape[2]))
    rotated = jnp.stack([own_block, jnp.stack([own_block[:, 1], -own_block[:, 0]], 1)], 0)
    cross_spectra = jnp.einsum('oicsf,jcsf->ofij', rotated.astype(jnp.float32), partner_block.astype(jnp.float32), precision=lax.Precision.HIGHEST).astype(jnp.bfloat16)
    lag_sums = jnp.einsum('ofij,ofl->ijl', cross_spectra.astype(jnp.float32), transform.astype(jnp.float32), precision=lax.Precision.HIGHEST)
    return (lag_sums * factor).astype(jnp.bfloat16)

def reference(spectra, partners):
    whitened = whiten(spectra, SMOOTH)
    transform = lag_table(BINS)
    blocks = whitened.reshape(N_GRP, GRP_CH, 2, SEG, BINS)
    column_index = jnp.arange(GRP_CH, dtype=jnp.int32)
    member_slot = column_index // CH_DEV
    per_round = []
    for round_index in range(R_WIN):
        slot_offsets = partners[round_index][member_slot].astype(jnp.int32)

        def one_group(group_index):
            own_block = lax.dynamic_index_in_dim(blocks, group_index, 0, keepdims=False)
            partner_rows = jnp.bitwise_xor(group_index, slot_offsets) * GRP_CH + column_index
            partner_block = jnp.take(whitened, partner_rows.astype(jnp.int32), axis=0)
            return pair_lags(own_block, partner_block, transform)
        result = lax.map(one_group, jnp.arange(N_GRP, dtype=jnp.int32))
        per_round.append(result.reshape(NCH, GRP_CH, LAGS))
    return jnp.stack(per_round, 1)
```

```python
import functools
import math

import jax
import jax.numpy as jnp
import numpy as np
from jax import lax
from jax.experimental import pallas as pl
from jax.experimental.pallas import tpu as pltpu
from jax.sharding import PartitionSpec as P

SMOOTH = 32
FLOOR = 1e-05
MESH = pl.DeviceIdType.MESH

NZ = 4
CHUNKS = 2
OVER_XY = {0: (0, 1), 1: (1, 2), 2: (1, 2), 3: (2, 3)}
OWN, XCOL, YCOL, DIAG = (0, 0), (1, 0), (0, 1), (1, 1)


def from_partner(array, axis, distance):
    return lax.ppermute(array, axis, [(i, i ^ 1 << distance) for i in range(lax.axis_size(axis))])


def whiten(spectra, half_width):
    components = spectra.astype(jnp.float32)
    power_sum = components[:, 0] * components[:, 0] + components[:, 1] * components[:, 1]
    bin_count = power_sum.shape[-1]
    positions = jnp.arange(bin_count, dtype=jnp.int32)
    band_matrix = (jnp.abs(positions[:, None] - positions[None, :]) <= half_width).astype(
        jnp.float32
    )
    smooth = jnp.dot(power_sum.reshape(-1, bin_count), band_matrix, precision=lax.Precision.HIGHEST)
    smooth = smooth.reshape(power_sum.shape) / (2 * half_width + 1)
    inv_level = lax.rsqrt(smooth + FLOOR)
    return (components * inv_level[:, None]).astype(jnp.bfloat16)


def lag_table(bin_count):
    frequency = np.arange(bin_count)[:, None]
    lag_offset = np.arange(bin_count + 1)[None, :] - bin_count // 2
    angles = np.mod(frequency * lag_offset, 2 * bin_count) * (math.pi / bin_count)
    return np.stack([np.cos(angles), -np.sin(angles)], 0).astype(jnp.bfloat16)


def pair_lags(own_block, partner_block, transform):
    factor = math.sqrt(2.0 / (own_block.shape[3] * own_block.shape[2]))
    rotated = jnp.stack([own_block, jnp.stack([own_block[:, 1], -own_block[:, 0]], 1)], 0)
    cross_spectra = jnp.einsum(
        "oicsf,jcsf->ofij", rotated, partner_block, preferred_element_type=jnp.float32
    ).astype(jnp.bfloat16)
    lag_sums = jnp.einsum(
        "ofij,ofl->ijl", cross_spectra, transform, preferred_element_type=jnp.float32
    )
    return (lag_sums * factor).astype(jnp.bfloat16)


def route_shard(payload, offset, levels):
    for level in range(levels):
        swapped = from_partner(payload, "grp", level)
        payload = jnp.where(offset // 2**level % 2 == 1, swapped, payload)
    return payload


def any_mesh(spectra, partners):
    whitened = whiten(spectra, SMOOTH)
    transform = jnp.asarray(lag_table(spectra.shape[3]))
    member_index = lax.axis_index("mem")
    levels = lax.axis_size("grp").bit_length() - 1
    outputs = []
    for round_index in range(partners.shape[0]):
        source = route_shard(whitened, partners[round_index, member_index], levels)
        gathered = lax.all_gather(source, "mem", axis=0, tiled=True)
        outputs.append(pair_lags(whitened, gathered, transform))
    return jnp.stack(outputs, 1)


def forwards(z, column, plane, chunk):
    links = []
    if column == OWN:
        if plane >= z and z > 0:
            links.append("down")
        if plane <= z and z < NZ - 1:
            links.append("up")
        links += ["x", "y"]
    elif column == XCOL:
        if plane in OVER_XY[z] and chunk < CHUNKS // 2:
            links.append("y")
    elif column == YCOL:
        if plane in OVER_XY[z] and chunk >= CHUNKS // 2:
            links.append("x")
    else:
        if z > 0 and plane >= z and plane not in OVER_XY[z - 1]:
            links.append("down")
        if z < NZ - 1 and plane <= z and plane not in OVER_XY[z + 1]:
            links.append("up")
    return links


def arrivals():
    order = {z: [] for z in range(NZ)}
    waiting = {(z, link): [] for z in range(NZ) for link in ("up", "down", "x", "y")}

    def take(z, piece):
        for link in forwards(z, *piece):
            waiting[z, link].append(piece)

    for z in range(NZ):
        for chunk in range(CHUNKS):
            take(z, (OWN, z, chunk))
    while any(waiting.values()):
        landed = []
        for (z, link), queue in waiting.items():
            if queue:
                (dx, dy), plane, chunk = queue.pop(0)
                if link == "x":
                    landed.append((z, ((1 - dx, dy), plane, chunk)))
                elif link == "y":
                    landed.append((z, ((dx, 1 - dy), plane, chunk)))
                else:
                    step = 1 if link == "up" else -1
                    landed.append((z + step, ((dx, dy), plane, chunk)))
        for z, piece in landed:
            order[z].append(piece)
            take(z, piece)
    return order


def plan():
    steps = {}
    for z, pieces in arrivals().items():
        have = {(dy, plane): 0 for dy in (0, 1) for plane in range(NZ)}
        have[0, z] = CHUNKS
        steps[z], taken = [], []
        for piece in pieces:
            (dx, dy), plane, _ = piece
            taken.append(piece)
            have[dy, plane] += 1
            if have[dy, plane] == 2 * CHUNKS:
                steps[z].append((taken, plane * 2 + dy))
                taken = []
        assert not taken and len(steps[z]) == 2 * NZ
    return steps


def slice_kernel(
    partners_ref, spectra_ref, table_ref, out_ref,
    whole, bright, mine, mate, gathered, cross, send_sem, recv_sem, mate_send, mate_recv,
):
    channels, _, segments, bins = spectra_ref.shape
    lags = out_ref.shape[3]
    rows = segments * 2 * channels
    part = rows // CHUNKS
    grp, me = lax.axis_index("grp"), lax.axis_index("mem")
    x, y, z = me % 2, me // 2 % 2, me // 4
    target = {
        "x": (grp, me + 1 - 2 * x),
        "y": (grp, me + 2 - 4 * y),
        "up": (grp, me + 4),
        "down": (grp, me - 4),
        "mate": (1 - grp, me),
    }
    lane = {"x": 0, "y": 1, "up": 2, "down": 3}

    barrier = pltpu.get_barrier_semaphore()

    def greet(name):
        pl.semaphore_signal(barrier, inc=1, device_id=target[name], device_id_type=MESH)

    for name in ("mate", "x", "y"):
        greet(name)
    pl.when(z > 0)(lambda: greet("down"))
    pl.when(z < NZ - 1)(lambda: greet("up"))

    first = lax.broadcasted_iota(jnp.int32, (bins, bins), 0)
    second = lax.broadcasted_iota(jnp.int32, (bins, bins), 1)
    band = jnp.where(jnp.abs(first - second) <= SMOOTH, 1.0, 0.0).astype(jnp.bfloat16)
    values = spectra_ref[...].astype(jnp.float32)
    power = values[:, 0] * values[:, 0] + values[:, 1] * values[:, 1]
    power = power.reshape(channels * segments, bins)
    high = power.astype(jnp.bfloat16)
    low = (power - high.astype(jnp.float32)).astype(jnp.bfloat16)
    smooth = jnp.dot(high, band, preferred_element_type=jnp.float32)
    smooth += jnp.dot(low, band, preferred_element_type=jnp.float32)
    inverse = lax.rsqrt(smooth * (1.0 / (2 * SMOOTH + 1)) + FLOOR)
    inverse = inverse.reshape(channels, segments, bins)
    for channel in range(channels):
        for k in range(2):
            row = k * channels + channel
            white = spectra_ref[channel, k].astype(jnp.float32) * inverse[channel]
            for tile in range(bins // 128):
                at = pl.ds(row, segments, stride=2 * channels)
                whole[tile, at, :] = white[:, tile * 128 : (tile + 1) * 128]
    for tile in range(bins // 128):
        mine[:, tile * 128 : (tile + 1) * 128] = whole[tile].astype(jnp.bfloat16)

    pl.semaphore_wait(barrier, 3 + jnp.where(z > 0, 1, 0) + jnp.where(z < NZ - 1, 1, 0))

    def to_mate(chunk):
        piece = pl.ds(chunk * part, part)
        return pltpu.make_async_remote_copy(
            src_ref=mine.at[piece], dst_ref=mate.at[piece],
            send_sem=mate_send.at[chunk], recv_sem=mate_recv.at[chunk],
            device_id=target["mate"], device_id_type=MESH,
        )

    def member(column, plane):
        dx, dy = column
        return plane * 4 + (y if dy == 0 else 1 - y) * 2 + (x if dx == 0 else 1 - x)

    def copy(link, column, plane, chunk):
        slot = member(column, plane)
        piece = gathered.at[slot, pl.ds(chunk * part, part)]
        return pltpu.make_async_remote_copy(
            src_ref=piece, dst_ref=piece,
            send_sem=send_sem.at[lane[link], slot, chunk], recv_sem=recv_sem.at[slot, chunk],
            device_id=target[link], device_id_type=MESH,
        )

    def pass_on(zc, column, plane, chunk):
        for link in forwards(zc, column, plane, chunk):
            copy(link, column, plane, chunk).start()

    for chunk in range(CHUNKS):
        to_mate(chunk).start()
    other = partners_ref[0, me] % 2 == 1
    for chunk in range(CHUNKS):
        to_mate(chunk).wait_recv()
        piece = pl.ds(chunk * part, part)
        gathered[me, piece] = jnp.where(other, mate[piece], mine[piece])
        for zc in range(NZ):
            pl.when(z == zc)(functools.partial(pass_on, zc, OWN, zc, chunk))

    @pl.loop(0, segments)
    def _(segment):
        block = mine[pl.ds(pl.multiple_of(segment * 2 * channels, 16), 2 * channels)]
        block = block.astype(jnp.float32)
        for row in range(2 * channels):
            bright[segment, row] = jnp.broadcast_to(block[row : row + 1], (8, bins))

    steps = plan()
    factor = math.sqrt(2.0 / (bins * segments))

    def take(zc, pieces):
        for column, plane, chunk in pieces:
            copy("x", column, plane, chunk).wait_recv()
            pass_on(zc, column, plane, chunk)

    packed = 0
    for zc in range(NZ):
        number = sum(code * 8**index for index, (_, code) in enumerate(steps[zc]))
        packed = jnp.where(z == zc, number, packed)

    def step(index, packed):
        for zc in range(NZ):
            @pl.when(z == zc)
            def _():
                for number, (pieces, _) in enumerate(steps[zc]):
                    if pieces:
                        pl.when(index == number)(functools.partial(take, zc, pieces))

        code = packed % 8
        plane, dy = code // 2, code % 2
        pair = plane * 2 + y + dy - 2 * y * dy

        @pl.loop(0, bins // 128)
        def _(tile):
            lanes = pl.ds(pl.multiple_of(tile * 128, 128), 128)

            def add(segment, sums):
                sums = list(sums)
                at = pl.ds(pl.multiple_of(segment * 2 * channels, 16), 2 * channels)
                theirs = []
                for side in range(2):
                    block = gathered[pair * 2 + side, at, lanes].astype(jnp.float32)
                    theirs.append((block[:channels], block[channels:]))
                for i in range(channels):
                    real = bright[segment, i, :, lanes]
                    imag = bright[segment, channels + i, :, lanes]
                    for side, (b_real, b_imag) in enumerate(theirs):
                        at_sum = (i * 2 + side) * 2
                        sums[at_sum] += real * b_real + imag * b_imag
                        sums[at_sum + 1] += imag * b_real - real * b_imag
                return tuple(sums)

            zeros = tuple(jnp.zeros((8, 128), jnp.float32) for _ in range(4 * channels))
            sums = lax.fori_loop(0, segments, add, zeros)
            for i in range(channels):
                for o in range(2):
                    both = jnp.concatenate([sums[i * 4 + o], sums[i * 4 + 2 + o]], 0)
                    at = pl.ds(pl.multiple_of(tile * 128 + o * bins, 128), 128)
                    cross[i * 16 : (i + 1) * 16, at] = both.astype(jnp.bfloat16)

        result = jnp.dot(cross[...], table_ref[...], preferred_element_type=jnp.float32)
        result = (result * factor).astype(jnp.bfloat16)
        at = pl.ds(pl.multiple_of(pair * 16, 16), 16)
        for i in range(channels):
            out_ref[i, 0, at, :] = result[i * 16 : (i + 1) * 16, :lags]
        return packed // 8

    lax.fori_loop(0, 2 * NZ, step, packed)

    for chunk in range(CHUNKS):
        to_mate(chunk).wait_send()

    def drain(zc):
        pieces = [(OWN, zc, chunk) for chunk in range(CHUNKS)]
        pieces += [piece for taken, _ in steps[zc] for piece in taken]
        for piece in pieces:
            for link in forwards(zc, *piece):
                copy(link, *piece).wait_send()

    for zc in range(NZ):
        pl.when(z == zc)(functools.partial(drain, zc))


def on_slice(spectra, partners):
    channels, _, segments, bins = spectra.shape
    members = lax.axis_size("mem")
    rows = segments * 2 * channels
    lags = bins + 1
    wide = -(-lags // 128) * 128
    table = np.zeros((2 * bins, wide), jnp.bfloat16)
    table[:, :lags] = lag_table(bins).reshape(2 * bins, lags)
    vmem = pl.BlockSpec(memory_space=pltpu.VMEM)
    return pl.pallas_call(
        slice_kernel,
        out_shape=jax.ShapeDtypeStruct((channels, 1, members * channels, lags), jnp.bfloat16),
        in_specs=[pl.BlockSpec(memory_space=pltpu.SMEM), vmem, vmem],
        out_specs=vmem,
        scratch_shapes=[
            pltpu.VMEM((bins // 128, rows, 128), jnp.float32),
            pltpu.VMEM((segments, 2 * channels, 8, bins), jnp.float32),
            pltpu.VMEM((rows, bins), jnp.bfloat16),
            pltpu.VMEM((rows, bins), jnp.bfloat16),
            pltpu.VMEM((members, rows, bins), jnp.bfloat16),
            pltpu.VMEM((16 * channels, 2 * bins), jnp.bfloat16),
            pltpu.SemaphoreType.DMA((4, members, CHUNKS)),
            pltpu.SemaphoreType.DMA((members, CHUNKS)),
            pltpu.SemaphoreType.DMA((CHUNKS,)),
            pltpu.SemaphoreType.DMA((CHUNKS,)),
        ],
        compiler_params=pltpu.CompilerParams(
            collective_id=0, has_side_effects=True, vmem_limit_bytes=48 * 2**20
        ),
        cost_estimate=pl.CostEstimate(
            flops=2 * channels * members * channels * 2 * bins * lags,
            bytes_accessed=4 * 2**20,
            transcendentals=0,
        ),
    )(partners, spectra, jnp.asarray(table))


def solution(mesh):
    shape = (mesh.shape["grp"], mesh.shape["mem"])

    def on_device(spectra, partners):
        fits = spectra.shape == (8, 2, 16, 512) and partners.shape[0] == 1
        if shape == (2, 4 * NZ) and fits:
            return on_slice(spectra, partners)
        return any_mesh(spectra, partners)

    return jax.shard_map(
        on_device,
        mesh=mesh,
        in_specs=(P(("grp", "mem"), None, None, None), P()),
        out_specs=P(("grp", "mem"), None, None, None),
        check_vma=False,
    )
```

```python
import functools
import math

import jax
import jax.numpy as jnp
import numpy as np
from jax import lax
from jax.experimental import pallas as pl
from jax.experimental.pallas import tpu as pltpu
from jax.sharding import PartitionSpec as P

SMOOTH = 32
FLOOR = 1e-05
MESH = pl.DeviceIdType.MESH

NZ = 4
CHUNKS = 4
TILES = 4
SEND_TICKS, HOP_TICKS, TAKE_TICKS, TILE_TICKS, LAG_TICKS = 15, 8, 1, 4, 4
OVER_XY = {0: (0, 1), 1: (1, 2), 2: (1, 2), 3: (2, 3)}
OWN, XCOL, YCOL, DIAG = (0, 0), (1, 0), (0, 1), (1, 1)


def from_partner(array, axis, distance):
    return lax.ppermute(array, axis, [(i, i ^ 1 << distance) for i in range(lax.axis_size(axis))])


def whiten(spectra, half_width):
    components = spectra.astype(jnp.float32)
    power_sum = components[:, 0] * components[:, 0] + components[:, 1] * components[:, 1]
    bin_count = power_sum.shape[-1]
    positions = jnp.arange(bin_count, dtype=jnp.int32)
    band_matrix = (jnp.abs(positions[:, None] - positions[None, :]) <= half_width).astype(
        jnp.float32
    )
    smooth = jnp.dot(power_sum.reshape(-1, bin_count), band_matrix, precision=lax.Precision.HIGHEST)
    smooth = smooth.reshape(power_sum.shape) / (2 * half_width + 1)
    inv_level = lax.rsqrt(smooth + FLOOR)
    return (components * inv_level[:, None]).astype(jnp.bfloat16)


def lag_table(bin_count):
    frequency = np.arange(bin_count)[:, None]
    lag_offset = np.arange(bin_count + 1)[None, :] - bin_count // 2
    angles = np.mod(frequency * lag_offset, 2 * bin_count) * (math.pi / bin_count)
    return np.stack([np.cos(angles), -np.sin(angles)], 0).astype(jnp.bfloat16)


def pair_lags(own_block, partner_block, transform):
    factor = math.sqrt(2.0 / (own_block.shape[3] * own_block.shape[2]))
    rotated = jnp.stack([own_block, jnp.stack([own_block[:, 1], -own_block[:, 0]], 1)], 0)
    cross_spectra = jnp.einsum(
        "oicsf,jcsf->ofij", rotated, partner_block, preferred_element_type=jnp.float32
    ).astype(jnp.bfloat16)
    lag_sums = jnp.einsum(
        "ofij,ofl->ijl", cross_spectra, transform, preferred_element_type=jnp.float32
    )
    return (lag_sums * factor).astype(jnp.bfloat16)


def route_shard(payload, offset, levels):
    for level in range(levels):
        swapped = from_partner(payload, "grp", level)
        payload = jnp.where(offset // 2**level % 2 == 1, swapped, payload)
    return payload


def any_mesh(spectra, partners):
    whitened = whiten(spectra, SMOOTH)
    transform = jnp.asarray(lag_table(spectra.shape[3]))
    member_index = lax.axis_index("mem")
    levels = lax.axis_size("grp").bit_length() - 1
    outputs = []
    for round_index in range(partners.shape[0]):
        source = route_shard(whitened, partners[round_index, member_index], levels)
        gathered = lax.all_gather(source, "mem", axis=0, tiled=True)
        outputs.append(pair_lags(whitened, gathered, transform))
    return jnp.stack(outputs, 1)


def forwards(z, column, plane, chunk):
    links = []
    if column == OWN:
        if plane >= z and z > 0:
            links.append("down")
        if plane <= z and z < NZ - 1:
            links.append("up")
        links += ["x", "y"]
    elif column == XCOL:
        if plane in OVER_XY[z] and chunk < CHUNKS // 2:
            links.append("y")
    elif column == YCOL:
        if plane in OVER_XY[z] and chunk >= CHUNKS // 2:
            links.append("x")
    else:
        if z > 0 and plane >= z and plane not in OVER_XY[z - 1]:
            links.append("down")
        if z < NZ - 1 and plane <= z and plane not in OVER_XY[z + 1]:
            links.append("up")
    return links


def plan():
    links = {(z, link): [] for z in range(NZ) for link in ("up", "down", "x", "y")}
    landed = {z: [] for z in range(NZ)}
    have = {z: {(dy, plane): 0 for dy in (0, 1) for plane in range(NZ)} for z in range(NZ)}
    ready = {z: [] for z in range(NZ)}
    steps = {z: [] for z in range(NZ)}
    taken = {z: [] for z in range(NZ)}
    free = dict.fromkeys(range(NZ), 0)

    def take(z, piece, now):
        (_, dy), plane, _ = piece
        for link in forwards(z, *piece):
            links[z, link].append([piece, SEND_TICKS, now])
        have[z][dy, plane] += 1
        if have[z][dy, plane] == 2 * CHUNKS:
            ready[z].append((plane * 2 + dy, 0))

    for z in range(NZ):
        for chunk in range(CHUNKS):
            take(z, (OWN, z, chunk), 0)
    now = 0
    while any(len(done) < 2 * NZ or len(done[-1][1]) < TILES for done in steps.values()):
        for (z, link), queue in links.items():
            if queue and queue[0][2] <= now:
                queue[0][1] -= 1
                if queue[0][1] == 0:
                    (dx, dy), plane, chunk = queue.pop(0)[0]
                    if link == "x":
                        landed[z].append(((1 - dx, dy), plane, chunk, now + HOP_TICKS))
                    elif link == "y":
                        landed[z].append(((dx, 1 - dy), plane, chunk, now + HOP_TICKS))
                    else:
                        there = z + (1 if link == "up" else -1)
                        landed[there].append(((dx, dy), plane, chunk, now + HOP_TICKS))
        for z in range(NZ):
            if free[z] > now:
                continue
            if landed[z] and landed[z][0][3] <= now:
                piece = landed[z].pop(0)[:3]
                taken[z].append(piece)
                take(z, piece, now + TAKE_TICKS)
                free[z] = now + TAKE_TICKS
            elif ready[z]:
                code, tile = ready[z].pop(0)
                if tile == 0:
                    steps[z].append((code, []))
                steps[z][-1][1].append(taken[z])
                taken[z] = []
                free[z] = now + TILE_TICKS
                if tile + 1 < TILES:
                    ready[z].insert(0, (code, tile + 1))
                else:
                    free[z] += LAG_TICKS
        now += 1
    return steps


def slice_kernel(
    partners_ref, spectra_ref, table_ref, out_ref,
    whole, bright, mine, mate, gathered, cross, send_sem, recv_sem, mate_send, mate_recv,
):
    channels, _, segments, bins = spectra_ref.shape
    lags = out_ref.shape[3]
    rows = segments * 2 * channels
    part = rows // CHUNKS
    grp, me = lax.axis_index("grp"), lax.axis_index("mem")
    x, y, z = me % 2, me // 2 % 2, me // 4
    target = {
        "x": (grp, me + 1 - 2 * x),
        "y": (grp, me + 2 - 4 * y),
        "up": (grp, me + 4),
        "down": (grp, me - 4),
        "mate": (1 - grp, me),
    }
    lane = {"x": 0, "y": 1, "up": 2, "down": 3}

    barrier = pltpu.get_barrier_semaphore()

    def greet(name):
        pl.semaphore_signal(barrier, inc=1, device_id=target[name], device_id_type=MESH)

    for name in ("mate", "x", "y"):
        greet(name)
    pl.when(z > 0)(lambda: greet("down"))
    pl.when(z < NZ - 1)(lambda: greet("up"))

    first = lax.broadcasted_iota(jnp.int32, (bins, bins), 0)
    second = lax.broadcasted_iota(jnp.int32, (bins, bins), 1)
    band = jnp.where(jnp.abs(first - second) <= SMOOTH, 1.0, 0.0).astype(jnp.bfloat16)
    values = spectra_ref[...].astype(jnp.float32)
    power = values[:, 0] * values[:, 0] + values[:, 1] * values[:, 1]
    power = power.reshape(channels * segments, bins)
    high = power.astype(jnp.bfloat16)
    low = (power - high.astype(jnp.float32)).astype(jnp.bfloat16)
    smooth = jnp.dot(high, band, preferred_element_type=jnp.float32)
    smooth += jnp.dot(low, band, preferred_element_type=jnp.float32)
    inverse = lax.rsqrt(smooth * (1.0 / (2 * SMOOTH + 1)) + FLOOR)
    inverse = inverse.reshape(channels, segments, bins)
    for channel in range(channels):
        for k in range(2):
            row = k * channels + channel
            white = spectra_ref[channel, k].astype(jnp.float32) * inverse[channel]
            for tile in range(bins // 128):
                at = pl.ds(row, segments, stride=2 * channels)
                whole[tile, at, :] = white[:, tile * 128 : (tile + 1) * 128]
    for tile in range(bins // 128):
        mine[:, tile * 128 : (tile + 1) * 128] = whole[tile].astype(jnp.bfloat16)

    pl.semaphore_wait(barrier, 3 + jnp.where(z > 0, 1, 0) + jnp.where(z < NZ - 1, 1, 0))

    def to_mate(chunk):
        piece = pl.ds(chunk * part, part)
        return pltpu.make_async_remote_copy(
            src_ref=mine.at[piece], dst_ref=mate.at[piece],
            send_sem=mate_send.at[chunk], recv_sem=mate_recv.at[chunk],
            device_id=target["mate"], device_id_type=MESH,
        )

    def member(column, plane):
        dx, dy = column
        return plane * 4 + (y if dy == 0 else 1 - y) * 2 + (x if dx == 0 else 1 - x)

    def copy(link, column, plane, chunk):
        slot = member(column, plane)
        piece = gathered.at[slot, pl.ds(chunk * part, part)]
        return pltpu.make_async_remote_copy(
            src_ref=piece, dst_ref=piece,
            send_sem=send_sem.at[lane[link], slot, chunk], recv_sem=recv_sem.at[slot, chunk],
            device_id=target[link], device_id_type=MESH,
        )

    def pass_on(zc, column, plane, chunk):
        for link in forwards(zc, column, plane, chunk):
            copy(link, column, plane, chunk).start()

    for chunk in range(CHUNKS):
        to_mate(chunk).start()
    other = partners_ref[0, me] % 2 == 1
    for chunk in range(CHUNKS):
        to_mate(chunk).wait_recv()
        piece = pl.ds(chunk * part, part)
        gathered[me, piece] = jnp.where(other, mate[piece], mine[piece])
        for zc in range(NZ):
            pl.when(z == zc)(functools.partial(pass_on, zc, OWN, zc, chunk))

    @pl.loop(0, segments)
    def _(segment):
        block = mine[pl.ds(pl.multiple_of(segment * 2 * channels, 16), 2 * channels)]
        block = block.astype(jnp.float32)
        for row in range(2 * channels):
            bright[segment, row] = jnp.broadcast_to(block[row : row + 1], (8, bins))

    steps = plan()
    factor = math.sqrt(2.0 / (bins * segments))

    def take(zc, pieces):
        for column, plane, chunk in pieces:
            copy("x", column, plane, chunk).wait_recv()
            pass_on(zc, column, plane, chunk)

    packed = 0
    for zc in range(NZ):
        number = sum(code * 8**index for index, (code, _) in enumerate(steps[zc]))
        packed = jnp.where(z == zc, number, packed)

    def step(index, packed):
        code = packed % 8
        plane, dy = code // 2, code % 2
        pair = plane * 2 + y + dy - 2 * y * dy

        for tile in range(TILES):
            for zc in range(NZ):
                @pl.when(z == zc)
                def _():
                    for number, (_, pieces) in enumerate(steps[zc]):
                        if pieces[tile]:
                            pl.when(index == number)(functools.partial(take, zc, pieces[tile]))

            lanes = pl.ds(tile * 128, 128)

            def add(segment, sums):
                sums = list(sums)
                at = pl.ds(pl.multiple_of(segment * 2 * channels, 16), 2 * channels)
                theirs = []
                for side in range(2):
                    block = gathered[pair * 2 + side, at, lanes].astype(jnp.float32)
                    theirs.append((block[:channels], block[channels:]))
                for i in range(channels):
                    real = bright[segment, i, :, lanes]
                    imag = bright[segment, channels + i, :, lanes]
                    for side, (b_real, b_imag) in enumerate(theirs):
                        at_sum = (i * 2 + side) * 2
                        sums[at_sum] += real * b_real + imag * b_imag
                        sums[at_sum + 1] += imag * b_real - real * b_imag
                return tuple(sums)

            zeros = tuple(jnp.zeros((8, 128), jnp.float32) for _ in range(4 * channels))
            sums = lax.fori_loop(0, segments, add, zeros, unroll=4)
            for i in range(channels):
                for o in range(2):
                    both = jnp.concatenate([sums[i * 4 + o], sums[i * 4 + 2 + o]], 0)
                    at = pl.ds(tile * 128 + o * bins, 128)
                    cross[i * 16 : (i + 1) * 16, at] = both.astype(jnp.bfloat16)

        result = jnp.dot(cross[...], table_ref[...], preferred_element_type=jnp.float32)
        result = (result * factor).astype(jnp.bfloat16)
        at = pl.ds(pl.multiple_of(pair * 16, 16), 16)
        for i in range(channels):
            out_ref[i, 0, at, :] = result[i * 16 : (i + 1) * 16, :lags]
        return packed // 8

    lax.fori_loop(0, 2 * NZ, step, packed)

    for chunk in range(CHUNKS):
        to_mate(chunk).wait_send()

    def drain(zc):
        pieces = [(OWN, zc, chunk) for chunk in range(CHUNKS)]
        pieces += [piece for _, tiles in steps[zc] for taken in tiles for piece in taken]
        for piece in pieces:
            for link in forwards(zc, *piece):
                copy(link, *piece).wait_send()

    for zc in range(NZ):
        pl.when(z == zc)(functools.partial(drain, zc))


def on_slice(spectra, partners):
    channels, _, segments, bins = spectra.shape
    members = lax.axis_size("mem")
    rows = segments * 2 * channels
    lags = bins + 1
    wide = -(-lags // 128) * 128
    table = np.zeros((2 * bins, wide), jnp.bfloat16)
    table[:, :lags] = lag_table(bins).reshape(2 * bins, lags)
    vmem = pl.BlockSpec(memory_space=pltpu.VMEM)
    return pl.pallas_call(
        slice_kernel,
        out_shape=jax.ShapeDtypeStruct((channels, 1, members * channels, lags), jnp.bfloat16),
        in_specs=[pl.BlockSpec(memory_space=pltpu.SMEM), vmem, vmem],
        out_specs=vmem,
        scratch_shapes=[
            pltpu.VMEM((bins // 128, rows, 128), jnp.float32),
            pltpu.VMEM((segments, 2 * channels, 8, bins), jnp.float32),
            pltpu.VMEM((rows, bins), jnp.bfloat16),
            pltpu.VMEM((rows, bins), jnp.bfloat16),
            pltpu.VMEM((members, rows, bins), jnp.bfloat16),
            pltpu.VMEM((16 * channels, 2 * bins), jnp.bfloat16),
            pltpu.SemaphoreType.DMA((4, members, CHUNKS)),
            pltpu.SemaphoreType.DMA((members, CHUNKS)),
            pltpu.SemaphoreType.DMA((CHUNKS,)),
            pltpu.SemaphoreType.DMA((CHUNKS,)),
        ],
        compiler_params=pltpu.CompilerParams(
            collective_id=0, has_side_effects=True, vmem_limit_bytes=48 * 2**20
        ),
        cost_estimate=pl.CostEstimate(
            flops=2 * channels * members * channels * 2 * bins * lags,
            bytes_accessed=4 * 2**20,
            transcendentals=0,
        ),
    )(partners, spectra, jnp.asarray(table))


def solution(mesh):
    shape = (mesh.shape["grp"], mesh.shape["mem"])

    def on_device(spectra, partners):
        fits = spectra.shape == (8, 2, 16, 512) and partners.shape[0] == 1
        if shape == (2, 4 * NZ) and fits:
            return on_slice(spectra, partners)
        return any_mesh(spectra, partners)

    return jax.shard_map(
        on_device,
        mesh=mesh,
        in_specs=(P(("grp", "mem"), None, None, None), P()),
        out_specs=P(("grp", "mem"), None, None, None),
        check_vma=False,
    )
```

```python
import functools
import math

import jax
import jax.numpy as jnp
import numpy as np
from jax import lax
from jax.experimental import pallas as pl
from jax.experimental.pallas import tpu as pltpu
from jax.sharding import PartitionSpec as P

SMOOTH = 32
FLOOR = 1e-05
MESH = pl.DeviceIdType.MESH

NZ = 4
CHUNKS = 2
TILES = 4
SEND_TICKS, HOP_TICKS, TAKE_TICKS, TILE_TICKS, LAG_TICKS = 28, 8, 1, 4, 4
OVER_XY = {0: (0, 1), 1: (1, 2), 2: (1, 2), 3: (2, 3)}
OWN, XCOL, YCOL, DIAG = (0, 0), (1, 0), (0, 1), (1, 1)


def from_partner(array, axis, distance):
    return lax.ppermute(array, axis, [(i, i ^ 1 << distance) for i in range(lax.axis_size(axis))])


def whiten(spectra, half_width):
    components = spectra.astype(jnp.float32)
    power_sum = components[:, 0] * components[:, 0] + components[:, 1] * components[:, 1]
    bin_count = power_sum.shape[-1]
    positions = jnp.arange(bin_count, dtype=jnp.int32)
    band_matrix = (jnp.abs(positions[:, None] - positions[None, :]) <= half_width).astype(
        jnp.float32
    )
    smooth = jnp.dot(power_sum.reshape(-1, bin_count), band_matrix, precision=lax.Precision.HIGHEST)
    smooth = smooth.reshape(power_sum.shape) / (2 * half_width + 1)
    inv_level = lax.rsqrt(smooth + FLOOR)
    return (components * inv_level[:, None]).astype(jnp.bfloat16)


def lag_table(bin_count):
    frequency = np.arange(bin_count)[:, None]
    lag_offset = np.arange(bin_count + 1)[None, :] - bin_count // 2
    angles = np.mod(frequency * lag_offset, 2 * bin_count) * (math.pi / bin_count)
    return np.stack([np.cos(angles), -np.sin(angles)], 0).astype(jnp.bfloat16)


def pair_lags(own_block, partner_block, transform):
    factor = math.sqrt(2.0 / (own_block.shape[3] * own_block.shape[2]))
    rotated = jnp.stack([own_block, jnp.stack([own_block[:, 1], -own_block[:, 0]], 1)], 0)
    cross_spectra = jnp.einsum(
        "oicsf,jcsf->ofij", rotated, partner_block, preferred_element_type=jnp.float32
    ).astype(jnp.bfloat16)
    lag_sums = jnp.einsum(
        "ofij,ofl->ijl", cross_spectra, transform, preferred_element_type=jnp.float32
    )
    return (lag_sums * factor).astype(jnp.bfloat16)


def route_shard(payload, offset, levels):
    for level in range(levels):
        swapped = from_partner(payload, "grp", level)
        payload = jnp.where(offset // 2**level % 2 == 1, swapped, payload)
    return payload


def any_mesh(spectra, partners):
    whitened = whiten(spectra, SMOOTH)
    transform = jnp.asarray(lag_table(spectra.shape[3]))
    member_index = lax.axis_index("mem")
    levels = lax.axis_size("grp").bit_length() - 1
    outputs = []
    for round_index in range(partners.shape[0]):
        source = route_shard(whitened, partners[round_index, member_index], levels)
        gathered = lax.all_gather(source, "mem", axis=0, tiled=True)
        outputs.append(pair_lags(whitened, gathered, transform))
    return jnp.stack(outputs, 1)


def forwards(z, column, plane, chunk):
    links = []
    if column == OWN:
        if plane >= z and z > 0:
            links.append("down")
        if plane <= z and z < NZ - 1:
            links.append("up")
        links += ["x", "y"]
    elif column == XCOL:
        if plane in OVER_XY[z] and chunk < CHUNKS // 2:
            links.append("y")
    elif column == YCOL:
        if plane in OVER_XY[z] and chunk >= CHUNKS // 2:
            links.append("x")
    else:
        if z > 0 and plane >= z and plane not in OVER_XY[z - 1]:
            links.append("down")
        if z < NZ - 1 and plane <= z and plane not in OVER_XY[z + 1]:
            links.append("up")
    return links


def plan():
    links = {(z, link): [] for z in range(NZ) for link in ("up", "down", "x", "y")}
    landed = {z: [] for z in range(NZ)}
    have = {z: {(dy, plane): 0 for dy in (0, 1) for plane in range(NZ)} for z in range(NZ)}
    ready = {z: [] for z in range(NZ)}
    steps = {z: [] for z in range(NZ)}
    taken = {z: [] for z in range(NZ)}
    free = dict.fromkeys(range(NZ), 0)

    def take(z, piece, now):
        (_, dy), plane, _ = piece
        for link in forwards(z, *piece):
            links[z, link].append([piece, SEND_TICKS, now])
        have[z][dy, plane] += 1
        if have[z][dy, plane] == 2 * CHUNKS:
            ready[z].append((plane * 2 + dy, 0))

    for z in range(NZ):
        for chunk in range(CHUNKS):
            take(z, (OWN, z, chunk), 0)
    now = 0
    while any(len(done) < 2 * NZ or len(done[-1][1]) < TILES for done in steps.values()):
        for (z, link), queue in links.items():
            if queue and queue[0][2] <= now:
                queue[0][1] -= 1
                if queue[0][1] == 0:
                    (dx, dy), plane, chunk = queue.pop(0)[0]
                    if link == "x":
                        landed[z].append(((1 - dx, dy), plane, chunk, now + HOP_TICKS))
                    elif link == "y":
                        landed[z].append(((dx, 1 - dy), plane, chunk, now + HOP_TICKS))
                    else:
                        there = z + (1 if link == "up" else -1)
                        landed[there].append(((dx, dy), plane, chunk, now + HOP_TICKS))
        for z in range(NZ):
            if free[z] > now:
                continue
            if landed[z] and landed[z][0][3] <= now:
                piece = landed[z].pop(0)[:3]
                taken[z].append(piece)
                take(z, piece, now + TAKE_TICKS)
                free[z] = now + TAKE_TICKS
            elif ready[z]:
                code, tile = ready[z].pop(0)
                if tile == 0:
                    steps[z].append((code, []))
                steps[z][-1][1].append(taken[z])
                taken[z] = []
                free[z] = now + TILE_TICKS
                if tile + 1 < TILES:
                    ready[z].insert(0, (code, tile + 1))
                else:
                    free[z] += LAG_TICKS
        now += 1
    return steps


def slice_kernel(
    partners_ref, spectra_hbm, table_hbm, out_ref,
    spectra_ref, table_ref, in_sem, whole, bright, mine, mate, gathered, cross, send_sem, recv_sem, mate_send, mate_recv,
):
    channels, _, segments, bins = spectra_hbm.shape
    lags = out_ref.shape[3]
    rows = segments * 2 * channels
    part = rows // CHUNKS
    grp, me = lax.axis_index("grp"), lax.axis_index("mem")
    x, y, z = me % 2, me // 2 % 2, me // 4
    target = {
        "x": (grp, me + 1 - 2 * x),
        "y": (grp, me + 2 - 4 * y),
        "up": (grp, me + 4),
        "down": (grp, me - 4),
        "mate": (1 - grp, me),
    }
    load_spectra = pltpu.make_async_copy(spectra_hbm, spectra_ref, in_sem.at[0])
    load_table = pltpu.make_async_copy(table_hbm, table_ref, in_sem.at[1])
    load_spectra.start()
    load_table.start()
    lane = {"x": 0, "y": 1, "up": 2, "down": 3}

    barrier = pltpu.get_barrier_semaphore()

    def greet(name):
        pl.semaphore_signal(barrier, inc=1, device_id=target[name], device_id_type=MESH)

    for name in ("mate", "x", "y"):
        greet(name)
    pl.when(z > 0)(lambda: greet("down"))
    pl.when(z < NZ - 1)(lambda: greet("up"))

    first = lax.broadcasted_iota(jnp.int32, (bins, bins), 0)
    second = lax.broadcasted_iota(jnp.int32, (bins, bins), 1)
    band = jnp.where(jnp.abs(first - second) <= SMOOTH, 1.0, 0.0).astype(jnp.bfloat16)
    load_spectra.wait()
    values = spectra_ref[...].astype(jnp.float32)
    power = values[:, 0] * values[:, 0] + values[:, 1] * values[:, 1]
    power = power.reshape(channels * segments, bins)
    high = power.astype(jnp.bfloat16)
    low = (power - high.astype(jnp.float32)).astype(jnp.bfloat16)
    smooth = jnp.dot(high, band, preferred_element_type=jnp.float32)
    smooth += jnp.dot(low, band, preferred_element_type=jnp.float32)
    inverse = lax.rsqrt(smooth * (1.0 / (2 * SMOOTH + 1)) + FLOOR)
    inverse = inverse.reshape(channels, segments, bins)
    for channel in range(channels):
        for k in range(2):
            row = k * channels + channel
            white = spectra_ref[channel, k].astype(jnp.float32) * inverse[channel]
            for tile in range(bins // 128):
                at = pl.ds(row, segments, stride=2 * channels)
                whole[tile, at, :] = white[:, tile * 128 : (tile + 1) * 128]
    for tile in range(bins // 128):
        mine[:, tile * 128 : (tile + 1) * 128] = whole[tile].astype(jnp.bfloat16)

    pl.semaphore_wait(barrier, 3 + jnp.where(z > 0, 1, 0) + jnp.where(z < NZ - 1, 1, 0))

    def to_mate(chunk):
        piece = pl.ds(chunk * part, part)
        return pltpu.make_async_remote_copy(
            src_ref=mine.at[piece], dst_ref=mate.at[piece],
            send_sem=mate_send.at[chunk], recv_sem=mate_recv.at[chunk],
            device_id=target["mate"], device_id_type=MESH,
        )

    def member(column, plane):
        dx, dy = column
        return plane * 4 + (y if dy == 0 else 1 - y) * 2 + (x if dx == 0 else 1 - x)

    def copy(link, column, plane, chunk):
        slot = member(column, plane)
        piece = gathered.at[slot, pl.ds(chunk * part, part)]
        return pltpu.make_async_remote_copy(
            src_ref=piece, dst_ref=piece,
            send_sem=send_sem.at[lane[link], slot, chunk], recv_sem=recv_sem.at[slot, chunk],
            device_id=target[link], device_id_type=MESH,
        )

    def pass_on(zc, column, plane, chunk):
        for link in forwards(zc, column, plane, chunk):
            copy(link, column, plane, chunk).start()

    for chunk in range(CHUNKS):
        to_mate(chunk).start()
    other = partners_ref[0, me] % 2 == 1
    for chunk in range(CHUNKS):
        to_mate(chunk).wait_recv()
        piece = pl.ds(chunk * part, part)
        gathered[me, piece] = jnp.where(other, mate[piece], mine[piece])
        for zc in range(NZ):
            pl.when(z == zc)(functools.partial(pass_on, zc, OWN, zc, chunk))

    @pl.loop(0, segments)
    def _(segment):
        block = mine[pl.ds(pl.multiple_of(segment * 2 * channels, 16), 2 * channels)]
        block = block.astype(jnp.float32)
        for row in range(2 * channels):
            bright[segment, row] = jnp.broadcast_to(block[row : row + 1], (8, bins))

    load_table.wait()
    steps = plan()
    factor = math.sqrt(2.0 / (bins * segments))

    def take(zc, pieces):
        for column, plane, chunk in pieces:
            copy("x", column, plane, chunk).wait_recv()
            pass_on(zc, column, plane, chunk)

    packed = 0
    for zc in range(NZ):
        number = sum(code * 8**index for index, (code, _) in enumerate(steps[zc]))
        packed = jnp.where(z == zc, number, packed)

    def step(index, packed):
        code = packed % 8
        plane, dy = code // 2, code % 2
        pair = plane * 2 + y + dy - 2 * y * dy

        for tile in range(TILES):
            for zc in range(NZ):
                @pl.when(z == zc)
                def _():
                    for number, (_, pieces) in enumerate(steps[zc]):
                        if pieces[tile]:
                            pl.when(index == number)(functools.partial(take, zc, pieces[tile]))

            lanes = pl.ds(tile * 128, 128)

            def add(segment, sums):
                sums = list(sums)
                at = pl.ds(pl.multiple_of(segment * 2 * channels, 16), 2 * channels)
                theirs = []
                for side in range(2):
                    block = gathered[pair * 2 + side, at, lanes].astype(jnp.float32)
                    theirs.append((block[:channels], block[channels:]))
                for i in range(channels):
                    real = bright[segment, i, :, lanes]
                    imag = bright[segment, channels + i, :, lanes]
                    for side, (b_real, b_imag) in enumerate(theirs):
                        at_sum = (i * 2 + side) * 2
                        sums[at_sum] += real * b_real + imag * b_imag
                        sums[at_sum + 1] += imag * b_real - real * b_imag
                return tuple(sums)

            zeros = tuple(jnp.zeros((8, 128), jnp.float32) for _ in range(4 * channels))
            sums = lax.fori_loop(0, segments, add, zeros, unroll=4)
            for i in range(channels):
                for o in range(2):
                    both = jnp.concatenate([sums[i * 4 + o], sums[i * 4 + 2 + o]], 0)
                    at = pl.ds(tile * 128 + o * bins, 128)
                    cross[i * 16 : (i + 1) * 16, at] = both.astype(jnp.bfloat16)

        table = table_ref[...].reshape(2 * bins, -1)
        result = jnp.dot(cross[...], table, preferred_element_type=jnp.float32)
        result = (result * factor).astype(jnp.bfloat16)
        at = pl.ds(pl.multiple_of(pair * 16, 16), 16)
        for i in range(channels):
            out_ref[i, 0, at, :] = result[i * 16 : (i + 1) * 16, :lags]
        return packed // 8

    lax.fori_loop(0, 2 * NZ, step, packed)

    for chunk in range(CHUNKS):
        to_mate(chunk).wait_send()

    def drain(zc):
        pieces = [(OWN, zc, chunk) for chunk in range(CHUNKS)]
        pieces += [piece for _, tiles in steps[zc] for taken in tiles for piece in taken]
        for piece in pieces:
            for link in forwards(zc, *piece):
                copy(link, *piece).wait_send()

    for zc in range(NZ):
        pl.when(z == zc)(functools.partial(drain, zc))


def on_slice(spectra, partners):
    channels, _, segments, bins = spectra.shape
    members = lax.axis_size("mem")
    rows = segments * 2 * channels
    lags = bins + 1
    wide = -(-lags // 128) * 128
    table = np.zeros((2 * bins, wide), jnp.bfloat16)
    table[:, :lags] = lag_table(bins).reshape(2 * bins, lags)
    anywhere = pl.BlockSpec(memory_space=pl.ANY)
    vmem = pl.BlockSpec(memory_space=pltpu.VMEM)
    return pl.pallas_call(
        slice_kernel,
        out_shape=jax.ShapeDtypeStruct((channels, 1, members * channels, lags), jnp.bfloat16),
        in_specs=[pl.BlockSpec(memory_space=pltpu.SMEM), anywhere, anywhere],
        out_specs=vmem,
        scratch_shapes=[
            pltpu.VMEM(spectra.shape, jnp.bfloat16),
            pltpu.VMEM((2 * bins // 8, 8, wide), jnp.bfloat16),
            pltpu.SemaphoreType.DMA((2,)),
            pltpu.VMEM((bins // 128, rows, 128), jnp.float32),
            pltpu.VMEM((segments, 2 * channels, 8, bins), jnp.float32),
            pltpu.VMEM((rows, bins), jnp.bfloat16),
            pltpu.VMEM((rows, bins), jnp.bfloat16),
            pltpu.VMEM((members, rows, bins), jnp.bfloat16),
            pltpu.VMEM((16 * channels, 2 * bins), jnp.bfloat16),
            pltpu.SemaphoreType.DMA((4, members, CHUNKS)),
            pltpu.SemaphoreType.DMA((members, CHUNKS)),
            pltpu.SemaphoreType.DMA((CHUNKS,)),
            pltpu.SemaphoreType.DMA((CHUNKS,)),
        ],
        compiler_params=pltpu.CompilerParams(
            collective_id=0, has_side_effects=True, vmem_limit_bytes=60 * 2**20
        ),
        cost_estimate=pl.CostEstimate(
            flops=2 * channels * members * channels * 2 * bins * lags,
            bytes_accessed=4 * 2**20,
            transcendentals=0,
        ),
    )(partners, spectra, jnp.asarray(table.reshape(-1, 8, wide)))


def solution(mesh):
    shape = (mesh.shape["grp"], mesh.shape["mem"])

    def on_device(spectra, partners):
        fits = spectra.shape == (8, 2, 16, 512) and partners.shape[0] == 1
        if shape == (2, 4 * NZ) and fits:
            return on_slice(spectra, partners)
        return any_mesh(spectra, partners)

    return jax.shard_map(
        on_device,
        mesh=mesh,
        in_specs=(P(("grp", "mem"), None, None, None), P()),
        out_specs=P(("grp", "mem"), None, None, None),
        check_vma=False,
    )
```

```python
import functools
import math

import jax
import jax.numpy as jnp
import numpy as np
from jax import lax
from jax.experimental import pallas as pl
from jax.experimental.pallas import tpu as pltpu
from jax.sharding import PartitionSpec as P

SMOOTH = 32
FLOOR = 1e-05
MESH = pl.DeviceIdType.MESH

NZ = 4
CHUNKS = 2
TILES = 4
SEND_TICKS, HOP_TICKS, TAKE_TICKS, TILE_TICKS, LAG_TICKS = 28, 8, 1, 4, 4
OVER_XY = {0: (0, 1), 1: (1, 2), 2: (1, 2), 3: (2, 3)}
OWN, XCOL, YCOL, DIAG = (0, 0), (1, 0), (0, 1), (1, 1)


def from_partner(array, axis, distance):
    return lax.ppermute(array, axis, [(i, i ^ 1 << distance) for i in range(lax.axis_size(axis))])


def whiten(spectra, half_width):
    components = spectra.astype(jnp.float32)
    power_sum = components[:, 0] * components[:, 0] + components[:, 1] * components[:, 1]
    bin_count = power_sum.shape[-1]
    positions = jnp.arange(bin_count, dtype=jnp.int32)
    band_matrix = (jnp.abs(positions[:, None] - positions[None, :]) <= half_width).astype(
        jnp.float32
    )
    smooth = jnp.dot(power_sum.reshape(-1, bin_count), band_matrix, precision=lax.Precision.HIGHEST)
    smooth = smooth.reshape(power_sum.shape) / (2 * half_width + 1)
    inv_level = lax.rsqrt(smooth + FLOOR)
    return (components * inv_level[:, None]).astype(jnp.bfloat16)


def lag_table(bin_count):
    frequency = np.arange(bin_count)[:, None]
    lag_offset = np.arange(bin_count + 1)[None, :] - bin_count // 2
    angles = np.mod(frequency * lag_offset, 2 * bin_count) * (math.pi / bin_count)
    return np.stack([np.cos(angles), -np.sin(angles)], 0).astype(jnp.bfloat16)


def pair_lags(own_block, partner_block, transform):
    factor = math.sqrt(2.0 / (own_block.shape[3] * own_block.shape[2]))
    rotated = jnp.stack([own_block, jnp.stack([own_block[:, 1], -own_block[:, 0]], 1)], 0)
    cross_spectra = jnp.einsum(
        "oicsf,jcsf->ofij", rotated, partner_block, preferred_element_type=jnp.float32
    ).astype(jnp.bfloat16)
    lag_sums = jnp.einsum(
        "ofij,ofl->ijl", cross_spectra, transform, preferred_element_type=jnp.float32
    )
    return (lag_sums * factor).astype(jnp.bfloat16)


def route_shard(payload, offset, levels):
    for level in range(levels):
        swapped = from_partner(payload, "grp", level)
        payload = jnp.where(offset // 2**level % 2 == 1, swapped, payload)
    return payload


def any_mesh(spectra, partners):
    whitened = whiten(spectra, SMOOTH)
    transform = jnp.asarray(lag_table(spectra.shape[3]))
    member_index = lax.axis_index("mem")
    levels = lax.axis_size("grp").bit_length() - 1
    outputs = []
    for round_index in range(partners.shape[0]):
        source = route_shard(whitened, partners[round_index, member_index], levels)
        gathered = lax.all_gather(source, "mem", axis=0, tiled=True)
        outputs.append(pair_lags(whitened, gathered, transform))
    return jnp.stack(outputs, 1)


def forwards(z, column, plane, chunk):
    links = []
    if column == OWN:
        if plane >= z and z > 0:
            links.append("down")
        if plane <= z and z < NZ - 1:
            links.append("up")
        links += ["x", "y"]
    elif column == XCOL:
        if plane in OVER_XY[z] and chunk < CHUNKS // 2:
            links.append("y")
    elif column == YCOL:
        if plane in OVER_XY[z] and chunk >= CHUNKS // 2:
            links.append("x")
    else:
        if z > 0 and plane >= z and plane not in OVER_XY[z - 1]:
            links.append("down")
        if z < NZ - 1 and plane <= z and plane not in OVER_XY[z + 1]:
            links.append("up")
    return links


def plan():
    links = {(z, link): [] for z in range(NZ) for link in ("up", "down", "x", "y")}
    landed = {z: [] for z in range(NZ)}
    have = {z: {(dy, plane): 0 for dy in (0, 1) for plane in range(NZ)} for z in range(NZ)}
    ready = {z: [] for z in range(NZ)}
    steps = {z: [] for z in range(NZ)}
    taken = {z: [] for z in range(NZ)}
    free = dict.fromkeys(range(NZ), 0)

    def take(z, piece, now):
        (_, dy), plane, _ = piece
        for link in forwards(z, *piece):
            links[z, link].append([piece, SEND_TICKS, now])
        have[z][dy, plane] += 1
        if have[z][dy, plane] == 2 * CHUNKS:
            ready[z].append((plane * 2 + dy, 0))

    for z in range(NZ):
        for chunk in range(CHUNKS):
            take(z, (OWN, z, chunk), 0)
    now = 0
    while any(len(done) < 2 * NZ or len(done[-1][1]) < TILES for done in steps.values()):
        for (z, link), queue in links.items():
            if queue and queue[0][2] <= now:
                queue[0][1] -= 1
                if queue[0][1] == 0:
                    (dx, dy), plane, chunk = queue.pop(0)[0]
                    if link == "x":
                        landed[z].append(((1 - dx, dy), plane, chunk, now + HOP_TICKS))
                    elif link == "y":
                        landed[z].append(((dx, 1 - dy), plane, chunk, now + HOP_TICKS))
                    else:
                        there = z + (1 if link == "up" else -1)
                        landed[there].append(((dx, dy), plane, chunk, now + HOP_TICKS))
        for z in range(NZ):
            if free[z] > now:
                continue
            if landed[z] and landed[z][0][3] <= now:
                piece = landed[z].pop(0)[:3]
                taken[z].append(piece)
                take(z, piece, now + TAKE_TICKS)
                free[z] = now + TAKE_TICKS
            elif ready[z]:
                code, tile = ready[z].pop(0)
                if tile == 0:
                    steps[z].append((code, []))
                steps[z][-1][1].append(taken[z])
                taken[z] = []
                free[z] = now + TILE_TICKS
                if tile + 1 < TILES:
                    ready[z].insert(0, (code, tile + 1))
                else:
                    free[z] += LAG_TICKS
        now += 1
    return steps


def slice_kernel(
    partners_hbm, spectra_hbm, table_hbm, out_ref,
    partners_ref, spectra_ref, table_ref, in_sem, held, out_sem, whole, bright, mine, mate, gathered, cross, send_sem, recv_sem, mate_send, mate_recv,
):
    channels, _, segments, bins = spectra_hbm.shape
    lags = out_ref.shape[3]
    rows = segments * 2 * channels
    part = rows // CHUNKS
    grp, me = lax.axis_index("grp"), lax.axis_index("mem")
    x, y, z = me % 2, me // 2 % 2, me // 4
    target = {
        "x": (grp, me + 1 - 2 * x),
        "y": (grp, me + 2 - 4 * y),
        "up": (grp, me + 4),
        "down": (grp, me - 4),
        "mate": (1 - grp, me),
    }
    load_spectra = pltpu.make_async_copy(spectra_hbm, spectra_ref, in_sem.at[0])
    load_table = pltpu.make_async_copy(table_hbm, table_ref, in_sem.at[1])
    load_partners = pltpu.make_async_copy(partners_hbm, partners_ref, in_sem.at[2])
    load_spectra.start()
    load_partners.start()
    load_table.start()
    lane = {"x": 0, "y": 1, "up": 2, "down": 3}

    barrier = pltpu.get_barrier_semaphore()

    def greet(name):
        pl.semaphore_signal(barrier, inc=1, device_id=target[name], device_id_type=MESH)

    for name in ("mate", "x", "y"):
        greet(name)
    pl.when(z > 0)(lambda: greet("down"))
    pl.when(z < NZ - 1)(lambda: greet("up"))

    first = lax.broadcasted_iota(jnp.int32, (bins, bins), 0)
    second = lax.broadcasted_iota(jnp.int32, (bins, bins), 1)
    band = jnp.where(jnp.abs(first - second) <= SMOOTH, 1.0, 0.0).astype(jnp.bfloat16)
    def to_mate(chunk):
        piece = pl.ds(chunk * part, part)
        return pltpu.make_async_remote_copy(
            src_ref=mine.at[piece], dst_ref=mate.at[piece],
            send_sem=mate_send.at[chunk], recv_sem=mate_recv.at[chunk],
            device_id=target["mate"], device_id_type=MESH,
        )

    def member(column, plane):
        dx, dy = column
        return plane * 4 + (y if dy == 0 else 1 - y) * 2 + (x if dx == 0 else 1 - x)

    def copy(link, column, plane, chunk):
        slot = member(column, plane)
        piece = gathered.at[slot, pl.ds(chunk * part, part)]
        return pltpu.make_async_remote_copy(
            src_ref=piece, dst_ref=piece,
            send_sem=send_sem.at[lane[link], slot, chunk], recv_sem=recv_sem.at[slot, chunk],
            device_id=target[link], device_id_type=MESH,
        )

    def pass_on(zc, column, plane, chunk):
        for link in forwards(zc, column, plane, chunk):
            copy(link, column, plane, chunk).start()

    span = segments // CHUNKS

    def whiten_part(chunk):
        now = pl.ds(chunk * span, span)
        values = spectra_ref[:, :, now].astype(jnp.float32)
        power = values[:, 0] * values[:, 0] + values[:, 1] * values[:, 1]
        power = power.reshape(channels * span, bins)
        high = power.astype(jnp.bfloat16)
        low = (power - high.astype(jnp.float32)).astype(jnp.bfloat16)
        smooth = jnp.dot(high, band, preferred_element_type=jnp.float32)
        smooth += jnp.dot(low, band, preferred_element_type=jnp.float32)
        inverse = lax.rsqrt(smooth * (1.0 / (2 * SMOOTH + 1)) + FLOOR)
        inverse = inverse.reshape(channels, span, bins)
        for channel in range(channels):
            for k in range(2):
                white = values[channel, k] * inverse[channel]
                at = pl.ds(chunk * part + k * channels + channel, span, stride=2 * channels)
                for tile in range(bins // 128):
                    whole[tile, at, :] = white[:, tile * 128 : (tile + 1) * 128]
        at = pl.ds(chunk * part, part)
        for tile in range(bins // 128):
            mine[at, tile * 128 : (tile + 1) * 128] = whole[tile, at].astype(jnp.bfloat16)

    load_spectra.wait()
    for chunk in range(CHUNKS):
        whiten_part(chunk)
        if chunk == 0:
            neighbours = 3 + jnp.where(z > 0, 1, 0) + jnp.where(z < NZ - 1, 1, 0)
            pl.semaphore_wait(barrier, neighbours)
        to_mate(chunk).start()
    load_partners.wait()
    other = partners_ref[0, me] % 2 == 1
    for chunk in range(CHUNKS):
        to_mate(chunk).wait_recv()
        piece = pl.ds(chunk * part, part)
        gathered[me, piece] = jnp.where(other, mate[piece], mine[piece])
        for zc in range(NZ):
            pl.when(z == zc)(functools.partial(pass_on, zc, OWN, zc, chunk))

    @pl.loop(0, segments)
    def _(segment):
        block = mine[pl.ds(pl.multiple_of(segment * 2 * channels, 16), 2 * channels)]
        block = block.astype(jnp.float32)
        for row in range(2 * channels):
            bright[segment, row] = jnp.broadcast_to(block[row : row + 1], (8, bins))

    load_table.wait()
    steps = plan()
    factor = math.sqrt(2.0 / (bins * segments))

    def take(zc, pieces):
        for column, plane, chunk in pieces:
            copy("x", column, plane, chunk).wait_recv()
            pass_on(zc, column, plane, chunk)

    packed = 0
    for zc in range(NZ):
        number = sum(code * 8**index for index, (code, _) in enumerate(steps[zc]))
        packed = jnp.where(z == zc, number, packed)

    def step(index, packed):
        code = packed % 8
        plane, dy = code // 2, code % 2
        pair = plane * 2 + y + dy - 2 * y * dy

        for tile in range(TILES):
            for zc in range(NZ):
                @pl.when(z == zc)
                def _():
                    for number, (_, pieces) in enumerate(steps[zc]):
                        if pieces[tile]:
                            pl.when(index == number)(functools.partial(take, zc, pieces[tile]))

            lanes = pl.ds(tile * 128, 128)

            def add(segment, sums):
                sums = list(sums)
                at = pl.ds(pl.multiple_of(segment * 2 * channels, 16), 2 * channels)
                theirs = []
                for side in range(2):
                    block = gathered[pair * 2 + side, at, lanes].astype(jnp.float32)
                    theirs.append((block[:channels], block[channels:]))
                for i in range(channels):
                    real = bright[segment, i, :, lanes]
                    imag = bright[segment, channels + i, :, lanes]
                    for side, (b_real, b_imag) in enumerate(theirs):
                        at_sum = (i * 2 + side) * 2
                        sums[at_sum] += real * b_real + imag * b_imag
                        sums[at_sum + 1] += imag * b_real - real * b_imag
                return tuple(sums)

            zeros = tuple(jnp.zeros((8, 128), jnp.float32) for _ in range(4 * channels))
            sums = lax.fori_loop(0, segments, add, zeros, unroll=4)
            for i in range(channels):
                for o in range(2):
                    both = jnp.concatenate([sums[i * 4 + o], sums[i * 4 + 2 + o]], 0)
                    at = pl.ds(tile * 128 + o * bins, 128)
                    cross[i * 16 : (i + 1) * 16, at] = both.astype(jnp.bfloat16)

        table = table_ref[...].reshape(2 * bins, -1)
        result = jnp.dot(cross[...], table, preferred_element_type=jnp.float32)
        result = (result * factor).astype(jnp.bfloat16)
        for i in range(channels):
            held[pair, i] = result[i * 16 : (i + 1) * 16, :lags]
        to_out(pair).start()
        return packed // 8

    def to_out(pair):
        at = pl.ds(pl.multiple_of(pair * 16, 16), 16)
        return pltpu.make_async_copy(held.at[pair], out_ref.at[:, 0, at], out_sem.at[pair])

    lax.fori_loop(0, 2 * NZ, step, packed)
    for pair in range(2 * NZ):
        to_out(pair).wait()

    for chunk in range(CHUNKS):
        to_mate(chunk).wait_send()

    def drain(zc):
        pieces = [(OWN, zc, chunk) for chunk in range(CHUNKS)]
        pieces += [piece for _, tiles in steps[zc] for taken in tiles for piece in taken]
        for piece in pieces:
            for link in forwards(zc, *piece):
                copy(link, *piece).wait_send()

    for zc in range(NZ):
        pl.when(z == zc)(functools.partial(drain, zc))


def on_slice(spectra, partners):
    channels, _, segments, bins = spectra.shape
    members = lax.axis_size("mem")
    rows = segments * 2 * channels
    lags = bins + 1
    wide = -(-lags // 128) * 128
    table = np.zeros((2 * bins, wide), jnp.bfloat16)
    table[:, :lags] = lag_table(bins).reshape(2 * bins, lags)
    hbm = pl.BlockSpec(memory_space=pl.ANY)
    return pl.pallas_call(
        slice_kernel,
        out_shape=jax.ShapeDtypeStruct((channels, 1, members * channels, lags), jnp.bfloat16),
        in_specs=[hbm, hbm, hbm],
        out_specs=hbm,
        scratch_shapes=[
            pltpu.SMEM(partners.shape, jnp.int32),
            pltpu.VMEM(spectra.shape, jnp.bfloat16),
            pltpu.VMEM((2 * bins // 8, 8, wide), jnp.bfloat16),
            pltpu.SemaphoreType.DMA((3,)),
            pltpu.VMEM((members // 2, channels, 16, lags), jnp.bfloat16),
            pltpu.SemaphoreType.DMA((members // 2,)),
            pltpu.VMEM((bins // 128, rows, 128), jnp.float32),
            pltpu.VMEM((segments, 2 * channels, 8, bins), jnp.float32),
            pltpu.VMEM((rows, bins), jnp.bfloat16),
            pltpu.VMEM((rows, bins), jnp.bfloat16),
            pltpu.VMEM((members, rows, bins), jnp.bfloat16),
            pltpu.VMEM((16 * channels, 2 * bins), jnp.bfloat16),
            pltpu.SemaphoreType.DMA((4, members, CHUNKS)),
            pltpu.SemaphoreType.DMA((members, CHUNKS)),
            pltpu.SemaphoreType.DMA((CHUNKS,)),
            pltpu.SemaphoreType.DMA((CHUNKS,)),
        ],
        compiler_params=pltpu.CompilerParams(
            collective_id=0, has_side_effects=True, vmem_limit_bytes=60 * 2**20
        ),
        cost_estimate=pl.CostEstimate(
            flops=2 * channels * members * channels * 2 * bins * lags,
            bytes_accessed=4 * 2**20,
            transcendentals=0,
        ),
    )(partners, spectra, jnp.asarray(table.reshape(-1, 8, wide)))


def solution(mesh):
    shape = (mesh.shape["grp"], mesh.shape["mem"])

    def on_device(spectra, partners):
        fits = spectra.shape == (8, 2, 16, 512) and partners.shape[0] == 1
        if shape == (2, 4 * NZ) and fits:
            return on_slice(spectra, partners)
        return any_mesh(spectra, partners)

    return jax.shard_map(
        on_device,
        mesh=mesh,
        in_specs=(P(("grp", "mem"), None, None, None), P()),
        out_specs=P(("grp", "mem"), None, None, None),
        check_vma=False,
    )
```

```python
import functools
import math

import jax
import jax.numpy as jnp
import numpy as np
from jax import lax
from jax.experimental import pallas as pl
from jax.experimental.pallas import tpu as pltpu
from jax.sharding import PartitionSpec as P

SMOOTH = 32
FLOOR = 1e-05
MESH = pl.DeviceIdType.MESH

NZ = 4
CHUNKS = 2
TILES = 4
SEND_TICKS, HOP_TICKS, TAKE_TICKS, TILE_TICKS, LAG_TICKS = 28, 8, 1, 4, 6
OVER_XY = {0: (0, 1), 1: (1, 2), 2: (1, 2), 3: (2, 3)}
OWN, XCOL, YCOL, DIAG = (0, 0), (1, 0), (0, 1), (1, 1)


def from_partner(array, axis, distance):
    return lax.ppermute(array, axis, [(i, i ^ 1 << distance) for i in range(lax.axis_size(axis))])


def whiten(spectra, half_width):
    components = spectra.astype(jnp.float32)
    power_sum = components[:, 0] * components[:, 0] + components[:, 1] * components[:, 1]
    bin_count = power_sum.shape[-1]
    positions = jnp.arange(bin_count, dtype=jnp.int32)
    band_matrix = (jnp.abs(positions[:, None] - positions[None, :]) <= half_width).astype(
        jnp.float32
    )
    smooth = jnp.dot(power_sum.reshape(-1, bin_count), band_matrix, precision=lax.Precision.HIGHEST)
    smooth = smooth.reshape(power_sum.shape) / (2 * half_width + 1)
    inv_level = lax.rsqrt(smooth + FLOOR)
    return (components * inv_level[:, None]).astype(jnp.bfloat16)


def lag_table(bin_count):
    frequency = np.arange(bin_count)[:, None]
    lag_offset = np.arange(bin_count + 1)[None, :] - bin_count // 2
    angles = np.mod(frequency * lag_offset, 2 * bin_count) * (math.pi / bin_count)
    return np.stack([np.cos(angles), -np.sin(angles)], 0).astype(jnp.bfloat16)


def pair_lags(own_block, partner_block, transform):
    factor = math.sqrt(2.0 / (own_block.shape[3] * own_block.shape[2]))
    rotated = jnp.stack([own_block, jnp.stack([own_block[:, 1], -own_block[:, 0]], 1)], 0)
    cross_spectra = jnp.einsum(
        "oicsf,jcsf->ofij", rotated, partner_block, preferred_element_type=jnp.float32
    ).astype(jnp.bfloat16)
    lag_sums = jnp.einsum(
        "ofij,ofl->ijl", cross_spectra, transform, preferred_element_type=jnp.float32
    )
    return (lag_sums * factor).astype(jnp.bfloat16)


def route_shard(payload, offset, levels):
    for level in range(levels):
        swapped = from_partner(payload, "grp", level)
        payload = jnp.where(offset // 2**level % 2 == 1, swapped, payload)
    return payload


def any_mesh(spectra, partners):
    whitened = whiten(spectra, SMOOTH)
    transform = jnp.asarray(lag_table(spectra.shape[3]))
    member_index = lax.axis_index("mem")
    levels = lax.axis_size("grp").bit_length() - 1
    outputs = []
    for round_index in range(partners.shape[0]):
        source = route_shard(whitened, partners[round_index, member_index], levels)
        gathered = lax.all_gather(source, "mem", axis=0, tiled=True)
        outputs.append(pair_lags(whitened, gathered, transform))
    return jnp.stack(outputs, 1)


def forwards(z, column, plane, chunk):
    links = []
    if column == OWN:
        if plane >= z and z > 0:
            links.append("down")
        if plane <= z and z < NZ - 1:
            links.append("up")
        links += ["x", "y"]
    elif column == XCOL:
        if plane in OVER_XY[z] and chunk < CHUNKS // 2:
            links.append("y")
    elif column == YCOL:
        if plane in OVER_XY[z] and chunk >= CHUNKS // 2:
            links.append("x")
    else:
        if z > 0 and plane >= z and plane not in OVER_XY[z - 1]:
            links.append("down")
        if z < NZ - 1 and plane <= z and plane not in OVER_XY[z + 1]:
            links.append("up")
    return links


def plan():
    links = {(z, link): [] for z in range(NZ) for link in ("up", "down", "x", "y")}
    landed = {z: [] for z in range(NZ)}
    have = {z: {(dy, plane): 0 for dy in (0, 1) for plane in range(NZ)} for z in range(NZ)}
    ready = {z: [] for z in range(NZ)}
    steps = {z: [] for z in range(NZ)}
    taken = {z: [] for z in range(NZ)}
    free = dict.fromkeys(range(NZ), 0)

    def take(z, piece, now):
        (_, dy), plane, _ = piece
        for link in forwards(z, *piece):
            links[z, link].append([piece, SEND_TICKS, now])
        have[z][dy, plane] += 1
        if have[z][dy, plane] == 2 * CHUNKS:
            ready[z].append((plane * 2 + dy, 0))

    for z in range(NZ):
        for chunk in range(CHUNKS):
            take(z, (OWN, z, chunk), 0)
    now = 0
    while any(len(done) < 2 * NZ or len(done[-1][1]) < TILES for done in steps.values()):
        for (z, link), queue in links.items():
            if queue and queue[0][2] <= now:
                queue[0][1] -= 1
                if queue[0][1] == 0:
                    (dx, dy), plane, chunk = queue.pop(0)[0]
                    if link == "x":
                        landed[z].append(((1 - dx, dy), plane, chunk, now + HOP_TICKS))
                    elif link == "y":
                        landed[z].append(((dx, 1 - dy), plane, chunk, now + HOP_TICKS))
                    else:
                        there = z + (1 if link == "up" else -1)
                        landed[there].append(((dx, dy), plane, chunk, now + HOP_TICKS))
        for z in range(NZ):
            if free[z] > now:
                continue
            if landed[z] and landed[z][0][3] <= now:
                piece = landed[z].pop(0)[:3]
                taken[z].append(piece)
                take(z, piece, now + TAKE_TICKS)
                free[z] = now + TAKE_TICKS
            elif ready[z]:
                code, tile = ready[z].pop(0)
                if tile == 0:
                    steps[z].append((code, []))
                steps[z][-1][1].append(taken[z])
                taken[z] = []
                free[z] = now + TILE_TICKS
                if tile + 1 < TILES:
                    ready[z].insert(0, (code, tile + 1))
                elif len(steps[z]) % 2 == 0:
                    free[z] += LAG_TICKS
        now += 1
    return steps


def slice_kernel(
    partners_hbm, spectra_hbm, table_hbm, out_ref,
    partners_ref, spectra_ref, table_ref, in_sem, held, out_sem, whole, bright, mine, mate, gathered, cross, send_sem, recv_sem, mate_send, mate_recv,
):
    channels, _, segments, bins = spectra_hbm.shape
    lags = out_ref.shape[3]
    rows = segments * 2 * channels
    part = rows // CHUNKS
    grp, me = lax.axis_index("grp"), lax.axis_index("mem")
    x, y, z = me % 2, me // 2 % 2, me // 4
    target = {
        "x": (grp, me + 1 - 2 * x),
        "y": (grp, me + 2 - 4 * y),
        "up": (grp, me + 4),
        "down": (grp, me - 4),
        "mate": (1 - grp, me),
    }
    load_spectra = pltpu.make_async_copy(spectra_hbm, spectra_ref, in_sem.at[0])
    load_table = pltpu.make_async_copy(table_hbm, table_ref, in_sem.at[1])
    load_partners = pltpu.make_async_copy(partners_hbm, partners_ref, in_sem.at[2])
    load_spectra.start()
    load_partners.start()
    load_table.start()
    lane = {"x": 0, "y": 1, "up": 2, "down": 3}

    barrier = pltpu.get_barrier_semaphore()

    def greet(name):
        pl.semaphore_signal(barrier, inc=1, device_id=target[name], device_id_type=MESH)

    for name in ("mate", "x", "y"):
        greet(name)
    pl.when(z > 0)(lambda: greet("down"))
    pl.when(z < NZ - 1)(lambda: greet("up"))

    first = lax.broadcasted_iota(jnp.int32, (bins, bins), 0)
    second = lax.broadcasted_iota(jnp.int32, (bins, bins), 1)
    band = jnp.where(jnp.abs(first - second) <= SMOOTH, 1.0, 0.0).astype(jnp.bfloat16)
    def to_mate(chunk):
        piece = pl.ds(chunk * part, part)
        return pltpu.make_async_remote_copy(
            src_ref=mine.at[piece], dst_ref=mate.at[piece],
            send_sem=mate_send.at[chunk], recv_sem=mate_recv.at[chunk],
            device_id=target["mate"], device_id_type=MESH,
        )

    def member(column, plane):
        dx, dy = column
        return plane * 4 + (y if dy == 0 else 1 - y) * 2 + (x if dx == 0 else 1 - x)

    def copy(link, column, plane, chunk):
        slot = member(column, plane)
        piece = gathered.at[slot, pl.ds(chunk * part, part)]
        return pltpu.make_async_remote_copy(
            src_ref=piece, dst_ref=piece,
            send_sem=send_sem.at[lane[link], slot, chunk], recv_sem=recv_sem.at[slot, chunk],
            device_id=target[link], device_id_type=MESH,
        )

    def pass_on(zc, column, plane, chunk):
        for link in forwards(zc, column, plane, chunk):
            copy(link, column, plane, chunk).start()

    span = segments // CHUNKS

    def whiten_part(chunk):
        now = pl.ds(chunk * span, span)
        values = spectra_ref[:, :, now].astype(jnp.float32)
        power = values[:, 0] * values[:, 0] + values[:, 1] * values[:, 1]
        power = power.reshape(channels * span, bins)
        high = power.astype(jnp.bfloat16)
        low = (power - high.astype(jnp.float32)).astype(jnp.bfloat16)
        smooth = jnp.dot(high, band, preferred_element_type=jnp.float32)
        smooth += jnp.dot(low, band, preferred_element_type=jnp.float32)
        inverse = lax.rsqrt(smooth * (1.0 / (2 * SMOOTH + 1)) + FLOOR)
        inverse = inverse.reshape(channels, span, bins)
        for channel in range(channels):
            for k in range(2):
                white = values[channel, k] * inverse[channel]
                at = pl.ds(chunk * part + k * channels + channel, span, stride=2 * channels)
                for tile in range(bins // 128):
                    whole[tile, at, :] = white[:, tile * 128 : (tile + 1) * 128]
        at = pl.ds(chunk * part, part)
        for tile in range(bins // 128):
            mine[at, tile * 128 : (tile + 1) * 128] = whole[tile, at].astype(jnp.bfloat16)

    load_spectra.wait()
    for chunk in range(CHUNKS):
        whiten_part(chunk)
        if chunk == 0:
            neighbours = 3 + jnp.where(z > 0, 1, 0) + jnp.where(z < NZ - 1, 1, 0)
            pl.semaphore_wait(barrier, neighbours)
        to_mate(chunk).start()
    load_partners.wait()
    other = partners_ref[0, me] % 2 == 1
    for chunk in range(CHUNKS):
        to_mate(chunk).wait_recv()
        piece = pl.ds(chunk * part, part)
        gathered[me, piece] = jnp.where(other, mate[piece], mine[piece])
        for zc in range(NZ):
            pl.when(z == zc)(functools.partial(pass_on, zc, OWN, zc, chunk))

    @pl.loop(0, segments)
    def _(segment):
        block = mine[pl.ds(pl.multiple_of(segment * 2 * channels, 16), 2 * channels)]
        block = block.astype(jnp.float32)
        both = block[:channels] + block[channels:]
        for i in range(channels):
            rows_of = (block[i : i + 1], block[channels + i : channels + i + 1], both[i : i + 1])
            for place, row in enumerate(rows_of):
                bright[segment, i * 3 + place] = jnp.broadcast_to(row, (8, bins))

    load_table.wait()
    steps = plan()
    factor = math.sqrt(2.0 / (bins * segments))

    def take(zc, pieces):
        for column, plane, chunk in pieces:
            copy("x", column, plane, chunk).wait_recv()
            pass_on(zc, column, plane, chunk)

    packed = 0
    for zc in range(NZ):
        number = sum(code * 8**index for index, (code, _) in enumerate(steps[zc]))
        packed = jnp.where(z == zc, number, packed)

    def step(index, half, packed):
        code = packed % 8
        plane, dy = code // 2, code % 2
        pair = plane * 2 + y + dy - 2 * y * dy

        for tile in range(TILES):
            for zc in range(NZ):
                @pl.when(z == zc)
                def _():
                    for number, (_, pieces) in enumerate(steps[zc]):
                        if number % 2 == half and pieces[tile]:
                            pl.when(index == number)(functools.partial(take, zc, pieces[tile]))

            lanes = pl.ds(tile * 128, 128)

            for low in range(0, channels, channels // 2):
                own = range(low, low + channels // 2)

                def add(segment, sums):
                    sums = list(sums)
                    at = pl.ds(pl.multiple_of(segment * 2 * channels, 16), 2 * channels)
                    theirs = []
                    for side in range(2):
                        block = gathered[pair * 2 + side, at, lanes].astype(jnp.float32)
                        real, imag = block[:channels], block[channels:]
                        theirs.append((real, imag, real - imag))
                    place = 0
                    for i in own:
                        ours = [bright[segment, i * 3 + k, :, lanes] for k in range(3)]
                        for their in theirs:
                            for k in range(3):
                                sums[place] += ours[k] * their[k]
                                place += 1
                    return tuple(sums)

                zeros = tuple(jnp.zeros((8, 128), jnp.float32) for _ in range(3 * channels))
                sums = lax.fori_loop(0, segments, add, zeros, unroll=4)
                for number, i in enumerate(own):
                    left, right = sums[number * 6 : number * 6 + 3], sums[number * 6 + 3 : number * 6 + 6]
                    real = [part[0] + part[1] for part in (left, right)]
                    imag = [part[2] - part[0] + part[1] for part in (left, right)]
                    for o, both in enumerate((real, imag)):
                        at = pl.ds(tile * 128 + o * bins, 128)
                        cross[half, i * 16 : (i + 1) * 16, at] = jnp.concatenate(both, 0).astype(jnp.bfloat16)

        return pair

    def two_steps(index, packed):
        pairs = [step(index * 2 + half, half, packed // 8**half) for half in range(2)]
        table = table_ref[...].reshape(2 * bins, -1)
        left = cross[...].reshape(2 * channels * 16, 2 * bins)
        result = jnp.dot(left, table, preferred_element_type=jnp.float32)
        result = (result * factor).astype(jnp.bfloat16)
        for half, pair in enumerate(pairs):
            for i in range(channels):
                row = (half * channels + i) * 16
                held[pair, i] = result[row : row + 16, :lags]
            to_out(pair).start()
        return packed // 64

    def to_out(pair):
        at = pl.ds(pl.multiple_of(pair * 16, 16), 16)
        return pltpu.make_async_copy(held.at[pair], out_ref.at[:, 0, at], out_sem.at[pair])

    lax.fori_loop(0, NZ, two_steps, packed)
    for pair in range(2 * NZ):
        to_out(pair).wait()

    for chunk in range(CHUNKS):
        to_mate(chunk).wait_send()

    def drain(zc):
        pieces = [(OWN, zc, chunk) for chunk in range(CHUNKS)]
        pieces += [piece for _, tiles in steps[zc] for taken in tiles for piece in taken]
        for piece in pieces:
            for link in forwards(zc, *piece):
                copy(link, *piece).wait_send()

    for zc in range(NZ):
        pl.when(z == zc)(functools.partial(drain, zc))


def on_slice(spectra, partners):
    channels, _, segments, bins = spectra.shape
    members = lax.axis_size("mem")
    rows = segments * 2 * channels
    lags = bins + 1
    wide = -(-lags // 128) * 128
    table = np.zeros((2 * bins, wide), jnp.bfloat16)
    table[:, :lags] = lag_table(bins).reshape(2 * bins, lags)
    hbm = pl.BlockSpec(memory_space=pl.ANY)
    return pl.pallas_call(
        slice_kernel,
        out_shape=jax.ShapeDtypeStruct((channels, 1, members * channels, lags), jnp.bfloat16),
        in_specs=[hbm, hbm, hbm],
        out_specs=hbm,
        scratch_shapes=[
            pltpu.SMEM(partners.shape, jnp.int32),
            pltpu.VMEM(spectra.shape, jnp.bfloat16),
            pltpu.VMEM((2 * bins // 8, 8, wide), jnp.bfloat16),
            pltpu.SemaphoreType.DMA((3,)),
            pltpu.VMEM((members // 2, channels, 16, lags), jnp.bfloat16),
            pltpu.SemaphoreType.DMA((members // 2,)),
            pltpu.VMEM((bins // 128, rows, 128), jnp.float32),
            pltpu.VMEM((segments, 3 * channels, 8, bins), jnp.float32),
            pltpu.VMEM((rows, bins), jnp.bfloat16),
            pltpu.VMEM((rows, bins), jnp.bfloat16),
            pltpu.VMEM((members, rows, bins), jnp.bfloat16),
            pltpu.VMEM((2, 16 * channels, 2 * bins), jnp.bfloat16),
            pltpu.SemaphoreType.DMA((4, members, CHUNKS)),
            pltpu.SemaphoreType.DMA((members, CHUNKS)),
            pltpu.SemaphoreType.DMA((CHUNKS,)),
            pltpu.SemaphoreType.DMA((CHUNKS,)),
        ],
        compiler_params=pltpu.CompilerParams(
            collective_id=0, has_side_effects=True, vmem_limit_bytes=60 * 2**20
        ),
        cost_estimate=pl.CostEstimate(
            flops=2 * channels * members * channels * 2 * bins * lags,
            bytes_accessed=4 * 2**20,
            transcendentals=0,
        ),
    )(partners, spectra, jnp.asarray(table.reshape(-1, 8, wide)))


def solution(mesh):
    shape = (mesh.shape["grp"], mesh.shape["mem"])

    def on_device(spectra, partners):
        fits = spectra.shape == (8, 2, 16, 512) and partners.shape[0] == 1
        if shape == (2, 4 * NZ) and fits:
            return on_slice(spectra, partners)
        return any_mesh(spectra, partners)

    return jax.shard_map(
        on_device,
        mesh=mesh,
        in_specs=(P(("grp", "mem"), None, None, None), P()),
        out_specs=P(("grp", "mem"), None, None, None),
        check_vma=False,
    )
```

```python
import functools
import math

import jax
import jax.numpy as jnp
import numpy as np
from jax import lax
from jax.experimental import pallas as pl
from jax.experimental.pallas import tpu as pltpu
from jax.sharding import PartitionSpec as P

SMOOTH = 32
FLOOR = 1e-05
MESH = pl.DeviceIdType.MESH

NZ = 4
CHUNKS = 2
TILES = 4
SEND_TICKS, HOP_TICKS, TAKE_TICKS, TILE_TICKS, LAG_TICKS = 31, 8, 1, 4, 6
OWN, XCOL, YCOL, DIAG = (0, 0), (1, 0), (0, 1), (1, 1)
LINKS = {"x": "x", "y": "y", "u": "up", "d": "down"}
SOURCES = {
    0: {XCOL: "xx xx dx xx", YCOL: "yy yy yd yy", DIAG: "yx xy yx dd"},
    1: {XCOL: "uu xx xx dx", YCOL: "uu yy yy yd", DIAG: "uy yx dd xy"},
    2: {XCOL: "ux xx xx dd", YCOL: "yu yy yy dd", DIAG: "xy uu yx dy"},
    3: {XCOL: "xx ux xx xx", YCOL: "yy yu yy yy", DIAG: "uu yx xy yx"},
}


def from_partner(array, axis, distance):
    return lax.ppermute(array, axis, [(i, i ^ 1 << distance) for i in range(lax.axis_size(axis))])


def whiten(spectra, half_width):
    components = spectra.astype(jnp.float32)
    power_sum = components[:, 0] * components[:, 0] + components[:, 1] * components[:, 1]
    bin_count = power_sum.shape[-1]
    positions = jnp.arange(bin_count, dtype=jnp.int32)
    band_matrix = (jnp.abs(positions[:, None] - positions[None, :]) <= half_width).astype(
        jnp.float32
    )
    smooth = jnp.dot(power_sum.reshape(-1, bin_count), band_matrix, precision=lax.Precision.HIGHEST)
    smooth = smooth.reshape(power_sum.shape) / (2 * half_width + 1)
    inv_level = lax.rsqrt(smooth + FLOOR)
    return (components * inv_level[:, None]).astype(jnp.bfloat16)


def lag_table(bin_count):
    frequency = np.arange(bin_count)[:, None]
    lag_offset = np.arange(bin_count + 1)[None, :] - bin_count // 2
    angles = np.mod(frequency * lag_offset, 2 * bin_count) * (math.pi / bin_count)
    return np.stack([np.cos(angles), -np.sin(angles)], 0).astype(jnp.bfloat16)


def pair_lags(own_block, partner_block, transform):
    factor = math.sqrt(2.0 / (own_block.shape[3] * own_block.shape[2]))
    rotated = jnp.stack([own_block, jnp.stack([own_block[:, 1], -own_block[:, 0]], 1)], 0)
    cross_spectra = jnp.einsum(
        "oicsf,jcsf->ofij", rotated, partner_block, preferred_element_type=jnp.float32
    ).astype(jnp.bfloat16)
    lag_sums = jnp.einsum(
        "ofij,ofl->ijl", cross_spectra, transform, preferred_element_type=jnp.float32
    )
    return (lag_sums * factor).astype(jnp.bfloat16)


def route_shard(payload, offset, levels):
    for level in range(levels):
        swapped = from_partner(payload, "grp", level)
        payload = jnp.where(offset // 2**level % 2 == 1, swapped, payload)
    return payload


def any_mesh(spectra, partners):
    whitened = whiten(spectra, SMOOTH)
    transform = jnp.asarray(lag_table(spectra.shape[3]))
    member_index = lax.axis_index("mem")
    levels = lax.axis_size("grp").bit_length() - 1
    outputs = []
    for round_index in range(partners.shape[0]):
        source = route_shard(whitened, partners[round_index, member_index], levels)
        gathered = lax.all_gather(source, "mem", axis=0, tiled=True)
        outputs.append(pair_lags(whitened, gathered, transform))
    return jnp.stack(outputs, 1)


def source(z, column, plane, chunk):
    if column == OWN:
        return "down" if plane > z else "up" if plane < z else None
    return LINKS[SOURCES[z][column].split()[plane][chunk]]


def forwards(z, column, plane, chunk):
    dx, dy = column
    links = []
    if z > 0 and source(z - 1, column, plane, chunk) == "down":
        links.append("down")
    if z < NZ - 1 and source(z + 1, column, plane, chunk) == "up":
        links.append("up")
    if dx == 0 and source(z, (1, dy), plane, chunk) == "x":
        links.append("x")
    if dy == 0 and source(z, (dx, 1), plane, chunk) == "y":
        links.append("y")
    return links


def plan():
    links = {(z, link): [] for z in range(NZ) for link in ("up", "down", "x", "y")}
    landed = {z: [] for z in range(NZ)}
    have = {z: {(dy, plane): 0 for dy in (0, 1) for plane in range(NZ)} for z in range(NZ)}
    ready = {z: [] for z in range(NZ)}
    steps = {z: [] for z in range(NZ)}
    taken = {z: [] for z in range(NZ)}
    free = dict.fromkeys(range(NZ), 0)

    def take(z, piece, now):
        (_, dy), plane, _ = piece
        for link in forwards(z, *piece):
            links[z, link].append([piece, SEND_TICKS, now])
        have[z][dy, plane] += 1
        if have[z][dy, plane] == 2 * CHUNKS:
            ready[z].append((plane * 2 + dy, 0))

    for z in range(NZ):
        for chunk in range(CHUNKS):
            take(z, (OWN, z, chunk), 0)
    now = 0
    while any(len(done) < 2 * NZ or len(done[-1][1]) < TILES for done in steps.values()):
        for (z, link), queue in links.items():
            if queue and queue[0][2] <= now:
                queue[0][1] -= 1
                if queue[0][1] == 0:
                    (dx, dy), plane, chunk = queue.pop(0)[0]
                    if link == "x":
                        landed[z].append(((1 - dx, dy), plane, chunk, now + HOP_TICKS))
                    elif link == "y":
                        landed[z].append(((dx, 1 - dy), plane, chunk, now + HOP_TICKS))
                    else:
                        there = z + (1 if link == "up" else -1)
                        landed[there].append(((dx, dy), plane, chunk, now + HOP_TICKS))
        for z in range(NZ):
            if free[z] > now:
                continue
            if landed[z] and landed[z][0][3] <= now:
                piece = landed[z].pop(0)[:3]
                taken[z].append(piece)
                take(z, piece, now + TAKE_TICKS)
                free[z] = now + TAKE_TICKS
            elif ready[z]:
                code, tile = ready[z].pop(0)
                if tile == 0:
                    steps[z].append((code, []))
                steps[z][-1][1].append(taken[z])
                taken[z] = []
                free[z] = now + TILE_TICKS
                if tile + 1 < TILES:
                    ready[z].insert(0, (code, tile + 1))
                elif len(steps[z]) % 2 == 0:
                    free[z] += LAG_TICKS
        now += 1
    return steps


def slice_kernel(
    partners_hbm, spectra_hbm, table_hbm, out_ref,
    partners_ref, spectra_ref, table_ref, in_sem, held, out_sem, whole, bright, mine, mate, gathered, cross, send_sem, recv_sem, mate_send, mate_recv,
):
    channels, _, segments, bins = spectra_hbm.shape
    lags = out_ref.shape[3]
    rows = segments * 2 * channels
    part = rows // CHUNKS
    grp, me = lax.axis_index("grp"), lax.axis_index("mem")
    x, y, z = me % 2, me // 2 % 2, me // 4
    target = {
        "x": (grp, me + 1 - 2 * x),
        "y": (grp, me + 2 - 4 * y),
        "up": (grp, me + 4),
        "down": (grp, me - 4),
        "mate": (1 - grp, me),
    }
    load_spectra = pltpu.make_async_copy(spectra_hbm, spectra_ref, in_sem.at[0])
    load_table = pltpu.make_async_copy(table_hbm, table_ref, in_sem.at[1])
    load_partners = pltpu.make_async_copy(partners_hbm, partners_ref, in_sem.at[2])
    load_spectra.start()
    load_partners.start()
    load_table.start()
    lane = {"x": 0, "y": 1, "up": 2, "down": 3}

    barrier = pltpu.get_barrier_semaphore()

    def greet(name):
        pl.semaphore_signal(barrier, inc=1, device_id=target[name], device_id_type=MESH)

    for name in ("mate", "x", "y"):
        greet(name)
    pl.when(z > 0)(lambda: greet("down"))
    pl.when(z < NZ - 1)(lambda: greet("up"))

    first = lax.broadcasted_iota(jnp.int32, (bins, bins), 0)
    second = lax.broadcasted_iota(jnp.int32, (bins, bins), 1)
    band = jnp.where(jnp.abs(first - second) <= SMOOTH, 1.0, 0.0).astype(jnp.bfloat16)
    def to_mate(chunk):
        piece = pl.ds(chunk * part, part)
        return pltpu.make_async_remote_copy(
            src_ref=mine.at[piece], dst_ref=mate.at[piece],
            send_sem=mate_send.at[chunk], recv_sem=mate_recv.at[chunk],
            device_id=target["mate"], device_id_type=MESH,
        )

    def member(column, plane):
        dx, dy = column
        return plane * 4 + (y if dy == 0 else 1 - y) * 2 + (x if dx == 0 else 1 - x)

    def copy(link, column, plane, chunk):
        slot = member(column, plane)
        piece = gathered.at[slot, pl.ds(chunk * part, part)]
        return pltpu.make_async_remote_copy(
            src_ref=piece, dst_ref=piece,
            send_sem=send_sem.at[lane[link], slot, chunk], recv_sem=recv_sem.at[slot, chunk],
            device_id=target[link], device_id_type=MESH,
        )

    def pass_on(zc, column, plane, chunk):
        for link in forwards(zc, column, plane, chunk):
            copy(link, column, plane, chunk).start()

    span = segments // CHUNKS

    def whiten_part(chunk):
        now = pl.ds(chunk * span, span)
        values = spectra_ref[:, :, now].astype(jnp.float32)
        power = values[:, 0] * values[:, 0] + values[:, 1] * values[:, 1]
        power = power.reshape(channels * span, bins)
        high = power.astype(jnp.bfloat16)
        low = (power - high.astype(jnp.float32)).astype(jnp.bfloat16)
        smooth = jnp.dot(high, band, preferred_element_type=jnp.float32)
        smooth += jnp.dot(low, band, preferred_element_type=jnp.float32)
        inverse = lax.rsqrt(smooth * (1.0 / (2 * SMOOTH + 1)) + FLOOR)
        inverse = inverse.reshape(channels, span, bins)
        for channel in range(channels):
            for k in range(2):
                white = values[channel, k] * inverse[channel]
                at = pl.ds(chunk * part + k * channels + channel, span, stride=2 * channels)
                for tile in range(bins // 128):
                    whole[tile, at, :] = white[:, tile * 128 : (tile + 1) * 128]
        at = pl.ds(chunk * part, part)
        for tile in range(bins // 128):
            mine[at, tile * 128 : (tile + 1) * 128] = whole[tile, at].astype(jnp.bfloat16)

    load_spectra.wait()
    for chunk in range(CHUNKS):
        whiten_part(chunk)
        if chunk == 0:
            neighbours = 3 + jnp.where(z > 0, 1, 0) + jnp.where(z < NZ - 1, 1, 0)
            pl.semaphore_wait(barrier, neighbours)
        to_mate(chunk).start()
    load_partners.wait()
    other = partners_ref[0, me] % 2 == 1
    for chunk in range(CHUNKS):
        to_mate(chunk).wait_recv()
        piece = pl.ds(chunk * part, part)
        gathered[me, piece] = jnp.where(other, mate[piece], mine[piece])
        for zc in range(NZ):
            pl.when(z == zc)(functools.partial(pass_on, zc, OWN, zc, chunk))

    @pl.loop(0, segments)
    def _(segment):
        block = mine[pl.ds(pl.multiple_of(segment * 2 * channels, 16), 2 * channels)]
        block = block.astype(jnp.float32)
        both = block[:channels] + block[channels:]
        for i in range(channels):
            rows_of = (block[i : i + 1], block[channels + i : channels + i + 1], both[i : i + 1])
            for place, row in enumerate(rows_of):
                bright[segment, i * 3 + place] = jnp.broadcast_to(row, (8, bins))

    load_table.wait()
    steps = plan()
    factor = math.sqrt(2.0 / (bins * segments))

    def take(zc, pieces):
        for column, plane, chunk in pieces:
            copy("x", column, plane, chunk).wait_recv()
            pass_on(zc, column, plane, chunk)

    packed = 0
    for zc in range(NZ):
        number = sum(code * 8**index for index, (code, _) in enumerate(steps[zc]))
        packed = jnp.where(z == zc, number, packed)

    def step(index, half, packed):
        code = packed % 8
        plane, dy = code // 2, code % 2
        pair = plane * 2 + y + dy - 2 * y * dy

        for tile in range(TILES):
            for zc in range(NZ):
                @pl.when(z == zc)
                def _():
                    for number, (_, pieces) in enumerate(steps[zc]):
                        if number % 2 == half and pieces[tile]:
                            pl.when(index == number)(functools.partial(take, zc, pieces[tile]))

            lanes = pl.ds(tile * 128, 128)

            for low in range(0, channels, channels // 2):
                own = range(low, low + channels // 2)

                def add(segment, sums):
                    sums = list(sums)
                    at = pl.ds(pl.multiple_of(segment * 2 * channels, 16), 2 * channels)
                    theirs = []
                    for side in range(2):
                        block = gathered[pair * 2 + side, at, lanes].astype(jnp.float32)
                        real, imag = block[:channels], block[channels:]
                        theirs.append((real, imag, real - imag))
                    place = 0
                    for i in own:
                        ours = [bright[segment, i * 3 + k, :, lanes] for k in range(3)]
                        for their in theirs:
                            for k in range(3):
                                sums[place] += ours[k] * their[k]
                                place += 1
                    return tuple(sums)

                zeros = tuple(jnp.zeros((8, 128), jnp.float32) for _ in range(3 * channels))
                sums = lax.fori_loop(0, segments, add, zeros, unroll=4)
                for number, i in enumerate(own):
                    left, right = sums[number * 6 : number * 6 + 3], sums[number * 6 + 3 : number * 6 + 6]
                    real = [part[0] + part[1] for part in (left, right)]
                    imag = [part[2] - part[0] + part[1] for part in (left, right)]
                    for o, both in enumerate((real, imag)):
                        at = pl.ds(tile * 128 + o * bins, 128)
                        cross[half, i * 16 : (i + 1) * 16, at] = jnp.concatenate(both, 0).astype(jnp.bfloat16)

        return pair

    def two_steps(index, packed):
        pairs = [step(index * 2 + half, half, packed // 8**half) for half in range(2)]
        table = table_ref[...].reshape(2 * bins, -1)
        left = cross[...].reshape(2 * channels * 16, 2 * bins)
        result = jnp.dot(left, table, preferred_element_type=jnp.float32)
        result = (result * factor).astype(jnp.bfloat16)
        for half, pair in enumerate(pairs):
            for i in range(channels):
                row = (half * channels + i) * 16
                held[pair, i] = result[row : row + 16, :lags]
            to_out(pair).start()
        return packed // 64

    def to_out(pair):
        at = pl.ds(pl.multiple_of(pair * 16, 16), 16)
        return pltpu.make_async_copy(held.at[pair], out_ref.at[:, 0, at], out_sem.at[pair])

    lax.fori_loop(0, NZ, two_steps, packed)
    for pair in range(2 * NZ):
        to_out(pair).wait()

    for chunk in range(CHUNKS):
        to_mate(chunk).wait_send()

    def drain(zc):
        pieces = [(OWN, zc, chunk) for chunk in range(CHUNKS)]
        pieces += [piece for _, tiles in steps[zc] for taken in tiles for piece in taken]
        for piece in pieces:
            for link in forwards(zc, *piece):
                copy(link, *piece).wait_send()

    for zc in range(NZ):
        pl.when(z == zc)(functools.partial(drain, zc))


def on_slice(spectra, partners):
    channels, _, segments, bins = spectra.shape
    members = lax.axis_size("mem")
    rows = segments * 2 * channels
    lags = bins + 1
    wide = -(-lags // 128) * 128
    table = np.zeros((2 * bins, wide), jnp.bfloat16)
    table[:, :lags] = lag_table(bins).reshape(2 * bins, lags)
    hbm = pl.BlockSpec(memory_space=pl.ANY)
    return pl.pallas_call(
        slice_kernel,
        out_shape=jax.ShapeDtypeStruct((channels, 1, members * channels, lags), jnp.bfloat16),
        in_specs=[hbm, hbm, hbm],
        out_specs=hbm,
        scratch_shapes=[
            pltpu.SMEM(partners.shape, jnp.int32),
            pltpu.VMEM(spectra.shape, jnp.bfloat16),
            pltpu.VMEM((2 * bins // 8, 8, wide), jnp.bfloat16),
            pltpu.SemaphoreType.DMA((3,)),
            pltpu.VMEM((members // 2, channels, 16, lags), jnp.bfloat16),
            pltpu.SemaphoreType.DMA((members // 2,)),
            pltpu.VMEM((bins // 128, rows, 128), jnp.float32),
            pltpu.VMEM((segments, 3 * channels, 8, bins), jnp.float32),
            pltpu.VMEM((rows, bins), jnp.bfloat16),
            pltpu.VMEM((rows, bins), jnp.bfloat16),
            pltpu.VMEM((members, rows, bins), jnp.bfloat16),
            pltpu.VMEM((2, 16 * channels, 2 * bins), jnp.bfloat16),
            pltpu.SemaphoreType.DMA((4, members, CHUNKS)),
            pltpu.SemaphoreType.DMA((members, CHUNKS)),
            pltpu.SemaphoreType.DMA((CHUNKS,)),
            pltpu.SemaphoreType.DMA((CHUNKS,)),
        ],
        compiler_params=pltpu.CompilerParams(
            collective_id=0, has_side_effects=True, vmem_limit_bytes=60 * 2**20
        ),
        cost_estimate=pl.CostEstimate(
            flops=2 * channels * members * channels * 2 * bins * lags,
            bytes_accessed=4 * 2**20,
            transcendentals=0,
        ),
    )(partners, spectra, jnp.asarray(table.reshape(-1, 8, wide)))


def solution(mesh):
    shape = (mesh.shape["grp"], mesh.shape["mem"])

    def on_device(spectra, partners):
        fits = spectra.shape == (8, 2, 16, 512) and partners.shape[0] == 1
        if shape == (2, 4 * NZ) and fits:
            return on_slice(spectra, partners)
        return any_mesh(spectra, partners)

    return jax.shard_map(
        on_device,
        mesh=mesh,
        in_specs=(P(("grp", "mem"), None, None, None), P()),
        out_specs=P(("grp", "mem"), None, None, None),
        check_vma=False,
    )
```

```python
import functools
import math

import jax
import jax.numpy as jnp
import numpy as np
from jax import lax
from jax.experimental import pallas as pl
from jax.experimental.pallas import tpu as pltpu
from jax.sharding import PartitionSpec as P

SMOOTH = 32
FLOOR = 1e-05
MESH = pl.DeviceIdType.MESH

NZ = 4
CHUNKS = 2
TILES = 4
SEND_TICKS, HOP_TICKS, TAKE_TICKS, TILE_TICKS, LAG_TICKS = 31, 8, 1, 4, 6
OWN, XCOL, YCOL, DIAG = (0, 0), (1, 0), (0, 1), (1, 1)
LINKS = {"x": "x", "y": "y", "u": "up", "d": "down"}
SOURCES = {
    0: {XCOL: "xx xx dx dx", YCOL: "yy yy yd yd", DIAG: "yx yx xy xy"},
    1: {XCOL: "xx xx xx dx", YCOL: "yy yy yy yd", DIAG: "uu xy dd xy"},
    2: {XCOL: "ux xx xx xx", YCOL: "yu yy yy yy", DIAG: "xy uu xy dd"},
    3: {XCOL: "ux ux xx xx", YCOL: "yu yu yy yy", DIAG: "xy xy yx yx"},
}


def from_partner(array, axis, distance):
    return lax.ppermute(array, axis, [(i, i ^ 1 << distance) for i in range(lax.axis_size(axis))])


def whiten(spectra, half_width):
    components = spectra.astype(jnp.float32)
    power_sum = components[:, 0] * components[:, 0] + components[:, 1] * components[:, 1]
    bin_count = power_sum.shape[-1]
    positions = jnp.arange(bin_count, dtype=jnp.int32)
    band_matrix = (jnp.abs(positions[:, None] - positions[None, :]) <= half_width).astype(
        jnp.float32
    )
    smooth = jnp.dot(power_sum.reshape(-1, bin_count), band_matrix, precision=lax.Precision.HIGHEST)
    smooth = smooth.reshape(power_sum.shape) / (2 * half_width + 1)
    inv_level = lax.rsqrt(smooth + FLOOR)
    return (components * inv_level[:, None]).astype(jnp.bfloat16)


def lag_table(bin_count):
    frequency = np.arange(bin_count)[:, None]
    lag_offset = np.arange(bin_count + 1)[None, :] - bin_count // 2
    angles = np.mod(frequency * lag_offset, 2 * bin_count) * (math.pi / bin_count)
    return np.stack([np.cos(angles), -np.sin(angles)], 0).astype(jnp.bfloat16)


def pair_lags(own_block, partner_block, transform):
    factor = math.sqrt(2.0 / (own_block.shape[3] * own_block.shape[2]))
    rotated = jnp.stack([own_block, jnp.stack([own_block[:, 1], -own_block[:, 0]], 1)], 0)
    cross_spectra = jnp.einsum(
        "oicsf,jcsf->ofij", rotated, partner_block, preferred_element_type=jnp.float32
    ).astype(jnp.bfloat16)
    lag_sums = jnp.einsum(
        "ofij,ofl->ijl", cross_spectra, transform, preferred_element_type=jnp.float32
    )
    return (lag_sums * factor).astype(jnp.bfloat16)


def route_shard(payload, offset, levels):
    for level in range(levels):
        swapped = from_partner(payload, "grp", level)
        payload = jnp.where(offset // 2**level % 2 == 1, swapped, payload)
    return payload


def any_mesh(spectra, partners):
    whitened = whiten(spectra, SMOOTH)
    transform = jnp.asarray(lag_table(spectra.shape[3]))
    member_index = lax.axis_index("mem")
    levels = lax.axis_size("grp").bit_length() - 1
    outputs = []
    for round_index in range(partners.shape[0]):
        source = route_shard(whitened, partners[round_index, member_index], levels)
        gathered = lax.all_gather(source, "mem", axis=0, tiled=True)
        outputs.append(pair_lags(whitened, gathered, transform))
    return jnp.stack(outputs, 1)


def source(z, column, plane, chunk):
    if column == OWN:
        return "down" if plane > z else "up" if plane < z else None
    return LINKS[SOURCES[z][column].split()[plane][chunk]]


def forwards(z, column, plane, chunk):
    dx, dy = column
    links = []
    if z > 0 and source(z - 1, column, plane, chunk) == "down":
        links.append("down")
    if z < NZ - 1 and source(z + 1, column, plane, chunk) == "up":
        links.append("up")
    if dx == 0 and source(z, (1, dy), plane, chunk) == "x":
        links.append("x")
    if dy == 0 and source(z, (dx, 1), plane, chunk) == "y":
        links.append("y")
    return links


def plan():
    links = {(z, link): [] for z in range(NZ) for link in ("up", "down", "x", "y")}
    landed = {z: [] for z in range(NZ)}
    have = {z: {(dy, plane): 0 for dy in (0, 1) for plane in range(NZ)} for z in range(NZ)}
    ready = {z: [] for z in range(NZ)}
    steps = {z: [] for z in range(NZ)}
    taken = {z: [] for z in range(NZ)}
    free = dict.fromkeys(range(NZ), 0)

    def take(z, piece, now):
        (_, dy), plane, _ = piece
        for link in forwards(z, *piece):
            links[z, link].append([piece, SEND_TICKS, now])
        have[z][dy, plane] += 1
        if have[z][dy, plane] == 2 * CHUNKS:
            ready[z].append((plane * 2 + dy, 0))

    for z in range(NZ):
        for chunk in range(CHUNKS):
            take(z, (OWN, z, chunk), 0)
    now = 0
    while any(len(done) < 2 * NZ or len(done[-1][1]) < TILES for done in steps.values()):
        for (z, link), queue in links.items():
            if queue and queue[0][2] <= now:
                queue[0][1] -= 1
                if queue[0][1] == 0:
                    (dx, dy), plane, chunk = queue.pop(0)[0]
                    if link == "x":
                        landed[z].append(((1 - dx, dy), plane, chunk, now + HOP_TICKS))
                    elif link == "y":
                        landed[z].append(((dx, 1 - dy), plane, chunk, now + HOP_TICKS))
                    else:
                        there = z + (1 if link == "up" else -1)
                        landed[there].append(((dx, dy), plane, chunk, now + HOP_TICKS))
        for z in range(NZ):
            if free[z] > now:
                continue
            if landed[z] and landed[z][0][3] <= now:
                piece = landed[z].pop(0)[:3]
                taken[z].append(piece)
                take(z, piece, now + TAKE_TICKS)
                free[z] = now + TAKE_TICKS
            elif ready[z]:
                code, tile = ready[z].pop(0)
                if tile == 0:
                    steps[z].append((code, []))
                steps[z][-1][1].append(taken[z])
                taken[z] = []
                free[z] = now + TILE_TICKS
                if tile + 1 < TILES:
                    ready[z].insert(0, (code, tile + 1))
                elif len(steps[z]) % 2 == 0:
                    free[z] += LAG_TICKS
        now += 1
    return steps


def slice_kernel(
    partners_hbm, spectra_hbm, table_hbm, out_ref,
    partners_ref, spectra_ref, table_ref, in_sem, held, out_sem, whole, bright, mine, mate, gathered, cross, send_sem, recv_sem, mate_send, mate_recv,
):
    channels, _, segments, bins = spectra_hbm.shape
    lags = out_ref.shape[3]
    rows = segments * 2 * channels
    part = rows // CHUNKS
    grp, me = lax.axis_index("grp"), lax.axis_index("mem")
    x, y, z = me % 2, me // 2 % 2, me // 4
    target = {
        "x": (grp, me + 1 - 2 * x),
        "y": (grp, me + 2 - 4 * y),
        "up": (grp, me + 4),
        "down": (grp, me - 4),
        "mate": (1 - grp, me),
    }
    load_spectra = pltpu.make_async_copy(spectra_hbm, spectra_ref, in_sem.at[0])
    load_table = pltpu.make_async_copy(table_hbm, table_ref, in_sem.at[1])
    load_partners = pltpu.make_async_copy(partners_hbm, partners_ref, in_sem.at[2])
    load_spectra.start()
    load_partners.start()
    load_table.start()
    lane = {"x": 0, "y": 1, "up": 2, "down": 3}

    barrier = pltpu.get_barrier_semaphore()

    def greet(name):
        pl.semaphore_signal(barrier, inc=1, device_id=target[name], device_id_type=MESH)

    for name in ("mate", "x", "y"):
        greet(name)
    pl.when(z > 0)(lambda: greet("down"))
    pl.when(z < NZ - 1)(lambda: greet("up"))

    first = lax.broadcasted_iota(jnp.int32, (bins, bins), 0)
    second = lax.broadcasted_iota(jnp.int32, (bins, bins), 1)
    band = jnp.where(jnp.abs(first - second) <= SMOOTH, 1.0, 0.0).astype(jnp.bfloat16)
    def to_mate(chunk):
        piece = pl.ds(chunk * part, part)
        return pltpu.make_async_remote_copy(
            src_ref=mine.at[piece], dst_ref=mate.at[piece],
            send_sem=mate_send.at[chunk], recv_sem=mate_recv.at[chunk],
            device_id=target["mate"], device_id_type=MESH,
        )

    def member(column, plane):
        dx, dy = column
        return plane * 4 + (y if dy == 0 else 1 - y) * 2 + (x if dx == 0 else 1 - x)

    def copy(link, column, plane, chunk):
        slot = member(column, plane)
        piece = gathered.at[slot, pl.ds(chunk * part, part)]
        return pltpu.make_async_remote_copy(
            src_ref=piece, dst_ref=piece,
            send_sem=send_sem.at[lane[link], slot, chunk], recv_sem=recv_sem.at[slot, chunk],
            device_id=target[link], device_id_type=MESH,
        )

    def pass_on(zc, column, plane, chunk):
        for link in forwards(zc, column, plane, chunk):
            copy(link, column, plane, chunk).start()

    span = segments // CHUNKS

    def whiten_part(chunk):
        now = pl.ds(chunk * span, span)
        values = spectra_ref[:, :, now].astype(jnp.float32)
        power = values[:, 0] * values[:, 0] + values[:, 1] * values[:, 1]
        power = power.reshape(channels * span, bins)
        high = power.astype(jnp.bfloat16)
        low = (power - high.astype(jnp.float32)).astype(jnp.bfloat16)
        smooth = jnp.dot(high, band, preferred_element_type=jnp.float32)
        smooth += jnp.dot(low, band, preferred_element_type=jnp.float32)
        inverse = lax.rsqrt(smooth * (1.0 / (2 * SMOOTH + 1)) + FLOOR)
        inverse = inverse.reshape(channels, span, bins)
        for channel in range(channels):
            for k in range(2):
                white = values[channel, k] * inverse[channel]
                at = pl.ds(chunk * part + k * channels + channel, span, stride=2 * channels)
                for tile in range(bins // 128):
                    whole[tile, at, :] = white[:, tile * 128 : (tile + 1) * 128]
        at = pl.ds(chunk * part, part)
        for tile in range(bins // 128):
            mine[at, tile * 128 : (tile + 1) * 128] = whole[tile, at].astype(jnp.bfloat16)

    load_spectra.wait()
    for chunk in range(CHUNKS):
        whiten_part(chunk)
        if chunk == 0:
            neighbours = 3 + jnp.where(z > 0, 1, 0) + jnp.where(z < NZ - 1, 1, 0)
            pl.semaphore_wait(barrier, neighbours)
        to_mate(chunk).start()
    load_partners.wait()
    other = partners_ref[0, me] % 2 == 1
    for chunk in range(CHUNKS):
        to_mate(chunk).wait_recv()
        piece = pl.ds(chunk * part, part)
        gathered[me, piece] = jnp.where(other, mate[piece], mine[piece])
        for zc in range(NZ):
            pl.when(z == zc)(functools.partial(pass_on, zc, OWN, zc, chunk))

    @pl.loop(0, segments)
    def _(segment):
        block = mine[pl.ds(pl.multiple_of(segment * 2 * channels, 16), 2 * channels)]
        block = block.astype(jnp.float32)
        both = block[:channels] + block[channels:]
        for i in range(channels):
            rows_of = (block[i : i + 1], block[channels + i : channels + i + 1], both[i : i + 1])
            for place, row in enumerate(rows_of):
                bright[segment, i * 3 + place] = jnp.broadcast_to(row, (8, bins))

    load_table.wait()
    steps = plan()
    factor = math.sqrt(2.0 / (bins * segments))

    def take(zc, pieces):
        for column, plane, chunk in pieces:
            copy("x", column, plane, chunk).wait_recv()
            pass_on(zc, column, plane, chunk)

    packed = 0
    for zc in range(NZ):
        number = sum(code * 8**index for index, (code, _) in enumerate(steps[zc]))
        packed = jnp.where(z == zc, number, packed)

    def step(index, half, packed):
        code = packed % 8
        plane, dy = code // 2, code % 2
        pair = plane * 2 + y + dy - 2 * y * dy

        for tile in range(TILES):
            for zc in range(NZ):
                @pl.when(z == zc)
                def _():
                    for number, (_, pieces) in enumerate(steps[zc]):
                        if number % 2 == half and pieces[tile]:
                            pl.when(index == number)(functools.partial(take, zc, pieces[tile]))

            lanes = pl.ds(tile * 128, 128)

            for low in range(0, channels, channels // 2):
                own = range(low, low + channels // 2)

                def add(segment, sums):
                    sums = list(sums)
                    at = pl.ds(pl.multiple_of(segment * 2 * channels, 16), 2 * channels)
                    theirs = []
                    for side in range(2):
                        block = gathered[pair * 2 + side, at, lanes].astype(jnp.float32)
                        real, imag = block[:channels], block[channels:]
                        theirs.append((real, imag, real - imag))
                    place = 0
                    for i in own:
                        ours = [bright[segment, i * 3 + k, :, lanes] for k in range(3)]
                        for their in theirs:
                            for k in range(3):
                                sums[place] += ours[k] * their[k]
                                place += 1
                    return tuple(sums)

                zeros = tuple(jnp.zeros((8, 128), jnp.float32) for _ in range(3 * channels))
                sums = lax.fori_loop(0, segments, add, zeros, unroll=4)
                for number, i in enumerate(own):
                    left, right = sums[number * 6 : number * 6 + 3], sums[number * 6 + 3 : number * 6 + 6]
                    real = [part[0] + part[1] for part in (left, right)]
                    imag = [part[2] - part[0] + part[1] for part in (left, right)]
                    for o, both in enumerate((real, imag)):
                        at = pl.ds(tile * 128 + o * bins, 128)
                        cross[half, i * 16 : (i + 1) * 16, at] = jnp.concatenate(both, 0).astype(jnp.bfloat16)

        return pair

    def two_steps(index, packed):
        pairs = [step(index * 2 + half, half, packed // 8**half) for half in range(2)]
        table = table_ref[...].reshape(2 * bins, -1)
        left = cross[...].reshape(2 * channels * 16, 2 * bins)
        result = jnp.dot(left, table, preferred_element_type=jnp.float32)
        result = (result * factor).astype(jnp.bfloat16)
        for half, pair in enumerate(pairs):
            for i in range(channels):
                row = (half * channels + i) * 16
                held[pair, i] = result[row : row + 16, :lags]
            to_out(pair).start()
        return packed // 64

    def to_out(pair):
        at = pl.ds(pl.multiple_of(pair * 16, 16), 16)
        return pltpu.make_async_copy(held.at[pair], out_ref.at[:, 0, at], out_sem.at[pair])

    lax.fori_loop(0, NZ, two_steps, packed)
    for pair in range(2 * NZ):
        to_out(pair).wait()

    for chunk in range(CHUNKS):
        to_mate(chunk).wait_send()

    def drain(zc):
        pieces = [(OWN, zc, chunk) for chunk in range(CHUNKS)]
        pieces += [piece for _, tiles in steps[zc] for taken in tiles for piece in taken]
        for piece in pieces:
            for link in forwards(zc, *piece):
                copy(link, *piece).wait_send()

    for zc in range(NZ):
        pl.when(z == zc)(functools.partial(drain, zc))


def on_slice(spectra, partners):
    channels, _, segments, bins = spectra.shape
    members = lax.axis_size("mem")
    rows = segments * 2 * channels
    lags = bins + 1
    wide = -(-lags // 128) * 128
    table = np.zeros((2 * bins, wide), jnp.bfloat16)
    table[:, :lags] = lag_table(bins).reshape(2 * bins, lags)
    hbm = pl.BlockSpec(memory_space=pl.ANY)
    return pl.pallas_call(
        slice_kernel,
        out_shape=jax.ShapeDtypeStruct((channels, 1, members * channels, lags), jnp.bfloat16),
        in_specs=[hbm, hbm, hbm],
        out_specs=hbm,
        scratch_shapes=[
            pltpu.SMEM(partners.shape, jnp.int32),
            pltpu.VMEM(spectra.shape, jnp.bfloat16),
            pltpu.VMEM((2 * bins // 8, 8, wide), jnp.bfloat16),
            pltpu.SemaphoreType.DMA((3,)),
            pltpu.VMEM((members // 2, channels, 16, lags), jnp.bfloat16),
            pltpu.SemaphoreType.DMA((members // 2,)),
            pltpu.VMEM((bins // 128, rows, 128), jnp.float32),
            pltpu.VMEM((segments, 3 * channels, 8, bins), jnp.float32),
            pltpu.VMEM((rows, bins), jnp.bfloat16),
            pltpu.VMEM((rows, bins), jnp.bfloat16),
            pltpu.VMEM((members, rows, bins), jnp.bfloat16),
            pltpu.VMEM((2, 16 * channels, 2 * bins), jnp.bfloat16),
            pltpu.SemaphoreType.DMA((4, members, CHUNKS)),
            pltpu.SemaphoreType.DMA((members, CHUNKS)),
            pltpu.SemaphoreType.DMA((CHUNKS,)),
            pltpu.SemaphoreType.DMA((CHUNKS,)),
        ],
        compiler_params=pltpu.CompilerParams(
            collective_id=0, has_side_effects=True, vmem_limit_bytes=60 * 2**20
        ),
        cost_estimate=pl.CostEstimate(
            flops=2 * channels * members * channels * 2 * bins * lags,
            bytes_accessed=4 * 2**20,
            transcendentals=0,
        ),
    )(partners, spectra, jnp.asarray(table.reshape(-1, 8, wide)))


def solution(mesh):
    shape = (mesh.shape["grp"], mesh.shape["mem"])

    def on_device(spectra, partners):
        fits = spectra.shape == (8, 2, 16, 512) and partners.shape[0] == 1
        if shape == (2, 4 * NZ) and fits:
            return on_slice(spectra, partners)
        return any_mesh(spectra, partners)

    return jax.shard_map(
        on_device,
        mesh=mesh,
        in_specs=(P(("grp", "mem"), None, None, None), P()),
        out_specs=P(("grp", "mem"), None, None, None),
        check_vma=False,
    )
```

```python
import functools
import math

import jax
import jax.numpy as jnp
import numpy as np
from jax import lax
from jax.experimental import pallas as pl
from jax.experimental.pallas import tpu as pltpu
from jax.sharding import PartitionSpec as P

SMOOTH = 32
FLOOR = 1e-05
MESH = pl.DeviceIdType.MESH

NZ = 4
CHUNKS = 2
TILES = 4
SEND_TICKS, HOP_TICKS, TAKE_TICKS, TILE_TICKS, LAG_TICKS = 31, 8, 1, 4, 6
OWN, XCOL, YCOL, DIAG = (0, 0), (1, 0), (0, 1), (1, 1)
LINKS = {"x": "x", "y": "y", "u": "up", "d": "down"}
SOURCES = {
    0: {XCOL: "xx xx dx dx", YCOL: "yy yy yd yd", DIAG: "yx yx xy xy"},
    1: {XCOL: "xx xx xx dx", YCOL: "yy yy yy yd", DIAG: "uu xy dd xy"},
    2: {XCOL: "ux xx xx xx", YCOL: "yu yy yy yy", DIAG: "xy uu xy dd"},
    3: {XCOL: "ux ux xx xx", YCOL: "yu yu yy yy", DIAG: "xy xy yx yx"},
}


def from_partner(array, axis, distance):
    return lax.ppermute(array, axis, [(i, i ^ 1 << distance) for i in range(lax.axis_size(axis))])


def whiten(spectra, half_width):
    components = spectra.astype(jnp.float32)
    power_sum = components[:, 0] * components[:, 0] + components[:, 1] * components[:, 1]
    bin_count = power_sum.shape[-1]
    positions = jnp.arange(bin_count, dtype=jnp.int32)
    band_matrix = (jnp.abs(positions[:, None] - positions[None, :]) <= half_width).astype(
        jnp.float32
    )
    smooth = jnp.dot(power_sum.reshape(-1, bin_count), band_matrix, precision=lax.Precision.HIGHEST)
    smooth = smooth.reshape(power_sum.shape) / (2 * half_width + 1)
    inv_level = lax.rsqrt(smooth + FLOOR)
    return (components * inv_level[:, None]).astype(jnp.bfloat16)


def lag_table(bin_count):
    frequency = np.arange(bin_count)[:, None]
    lag_offset = np.arange(bin_count + 1)[None, :] - bin_count // 2
    angles = np.mod(frequency * lag_offset, 2 * bin_count) * (math.pi / bin_count)
    return np.stack([np.cos(angles), -np.sin(angles)], 0).astype(jnp.bfloat16)


def pair_lags(own_block, partner_block, transform):
    factor = math.sqrt(2.0 / (own_block.shape[3] * own_block.shape[2]))
    rotated = jnp.stack([own_block, jnp.stack([own_block[:, 1], -own_block[:, 0]], 1)], 0)
    cross_spectra = jnp.einsum(
        "oicsf,jcsf->ofij", rotated, partner_block, preferred_element_type=jnp.float32
    ).astype(jnp.bfloat16)
    lag_sums = jnp.einsum(
        "ofij,ofl->ijl", cross_spectra, transform, preferred_element_type=jnp.float32
    )
    return (lag_sums * factor).astype(jnp.bfloat16)


def route_shard(payload, offset, levels):
    for level in range(levels):
        swapped = from_partner(payload, "grp", level)
        payload = jnp.where(offset // 2**level % 2 == 1, swapped, payload)
    return payload


def any_mesh(spectra, partners):
    whitened = whiten(spectra, SMOOTH)
    transform = jnp.asarray(lag_table(spectra.shape[3]))
    member_index = lax.axis_index("mem")
    levels = lax.axis_size("grp").bit_length() - 1
    outputs = []
    for round_index in range(partners.shape[0]):
        source = route_shard(whitened, partners[round_index, member_index], levels)
        gathered = lax.all_gather(source, "mem", axis=0, tiled=True)
        outputs.append(pair_lags(whitened, gathered, transform))
    return jnp.stack(outputs, 1)


def source(z, column, plane, chunk):
    if column == OWN:
        return "down" if plane > z else "up" if plane < z else None
    return LINKS[SOURCES[z][column].split()[plane][chunk]]


def forwards(z, column, plane, chunk):
    dx, dy = column
    links = []
    if z > 0 and source(z - 1, column, plane, chunk) == "down":
        links.append("down")
    if z < NZ - 1 and source(z + 1, column, plane, chunk) == "up":
        links.append("up")
    if dx == 0 and source(z, (1, dy), plane, chunk) == "x":
        links.append("x")
    if dy == 0 and source(z, (dx, 1), plane, chunk) == "y":
        links.append("y")
    return links


def plan():
    links = {(z, link): [] for z in range(NZ) for link in ("up", "down", "x", "y")}
    landed = {z: [] for z in range(NZ)}
    have = {z: {(dy, plane): 0 for dy in (0, 1) for plane in range(NZ)} for z in range(NZ)}
    ready = {z: [] for z in range(NZ)}
    steps = {z: [] for z in range(NZ)}
    taken = {z: [] for z in range(NZ)}
    free = dict.fromkeys(range(NZ), 0)

    def take(z, piece, now):
        (_, dy), plane, _ = piece
        for link in forwards(z, *piece):
            links[z, link].append([piece, SEND_TICKS, now])
        have[z][dy, plane] += 1
        if have[z][dy, plane] == 2 * CHUNKS:
            ready[z].append((plane * 2 + dy, 0))

    for z in range(NZ):
        for chunk in range(CHUNKS):
            take(z, (OWN, z, chunk), 0)
    now = 0
    while any(len(done) < 2 * NZ or len(done[-1][1]) < TILES for done in steps.values()):
        for (z, link), queue in links.items():
            if queue and queue[0][2] <= now:
                queue[0][1] -= 1
                if queue[0][1] == 0:
                    (dx, dy), plane, chunk = queue.pop(0)[0]
                    if link == "x":
                        landed[z].append(((1 - dx, dy), plane, chunk, now + HOP_TICKS))
                    elif link == "y":
                        landed[z].append(((dx, 1 - dy), plane, chunk, now + HOP_TICKS))
                    else:
                        there = z + (1 if link == "up" else -1)
                        landed[there].append(((dx, dy), plane, chunk, now + HOP_TICKS))
        for z in range(NZ):
            if free[z] > now:
                continue
            if landed[z] and landed[z][0][3] <= now:
                piece = landed[z].pop(0)[:3]
                taken[z].append(piece)
                take(z, piece, now + TAKE_TICKS)
                free[z] = now + TAKE_TICKS
            elif ready[z]:
                code, tile = ready[z].pop(0)
                if tile == 0:
                    steps[z].append((code, []))
                steps[z][-1][1].append(taken[z])
                taken[z] = []
                free[z] = now + TILE_TICKS
                if tile + 1 < TILES:
                    ready[z].insert(0, (code, tile + 1))
                elif len(steps[z]) % 2 == 0:
                    free[z] += LAG_TICKS
        now += 1
    return steps


def slice_kernel(
    partners_hbm, spectra_hbm, table_hbm, out_ref,
    partners_ref, spectra_ref, table_ref, in_sem, held, out_sem, whole, bright, mine, mate, gathered, cross, send_sem, recv_sem, mate_send, mate_recv,
):
    channels, _, segments, bins = spectra_hbm.shape
    lags = out_ref.shape[3]
    rows = segments * 2 * channels
    part = rows // CHUNKS
    grp, me = lax.axis_index("grp"), lax.axis_index("mem")
    x, y, z = me % 2, me // 2 % 2, me // 4
    target = {
        "x": (grp, me + 1 - 2 * x),
        "y": (grp, me + 2 - 4 * y),
        "up": (grp, me + 4),
        "down": (grp, me - 4),
        "mate": (1 - grp, me),
    }
    load_spectra = pltpu.make_async_copy(spectra_hbm, spectra_ref, in_sem.at[0])
    load_table = pltpu.make_async_copy(table_hbm, table_ref, in_sem.at[1])
    load_partners = pltpu.make_async_copy(partners_hbm, partners_ref, in_sem.at[2])
    load_spectra.start()
    load_partners.start()
    load_table.start()
    lane = {"x": 0, "y": 1, "up": 2, "down": 3}

    barrier = pltpu.get_barrier_semaphore()

    def greet(name):
        pl.semaphore_signal(barrier, inc=1, device_id=target[name], device_id_type=MESH)

    for name in ("mate", "x", "y"):
        greet(name)
    pl.when(z > 0)(lambda: greet("down"))
    pl.when(z < NZ - 1)(lambda: greet("up"))

    first = lax.broadcasted_iota(jnp.int32, (bins, bins), 0)
    second = lax.broadcasted_iota(jnp.int32, (bins, bins), 1)
    band = jnp.where(jnp.abs(first - second) <= SMOOTH, 1.0, 0.0).astype(jnp.bfloat16)
    def to_mate(chunk):
        piece = pl.ds(chunk * part, part)
        return pltpu.make_async_remote_copy(
            src_ref=mine.at[piece], dst_ref=mate.at[piece],
            send_sem=mate_send.at[chunk], recv_sem=mate_recv.at[chunk],
            device_id=target["mate"], device_id_type=MESH,
        )

    def member(column, plane):
        dx, dy = column
        return plane * 4 + (y if dy == 0 else 1 - y) * 2 + (x if dx == 0 else 1 - x)

    def copy(link, column, plane, chunk):
        slot = member(column, plane)
        piece = gathered.at[slot, pl.ds(chunk * part, part)]
        return pltpu.make_async_remote_copy(
            src_ref=piece, dst_ref=piece,
            send_sem=send_sem.at[lane[link], slot, chunk], recv_sem=recv_sem.at[slot, chunk],
            device_id=target[link], device_id_type=MESH,
        )

    def pass_on(zc, column, plane, chunk):
        for link in forwards(zc, column, plane, chunk):
            copy(link, column, plane, chunk).start()

    span = segments // CHUNKS

    def whiten_part(chunk):
        values = spectra_ref[...].astype(jnp.float32)[:, :, chunk * span : (chunk + 1) * span]
        power = values[:, 0] * values[:, 0] + values[:, 1] * values[:, 1]
        power = power.reshape(channels * span, bins)
        high = power.astype(jnp.bfloat16)
        low = (power - high.astype(jnp.float32)).astype(jnp.bfloat16)
        smooth = jnp.dot(high, band, preferred_element_type=jnp.float32)
        smooth += jnp.dot(low, band, preferred_element_type=jnp.float32)
        inverse = lax.rsqrt(smooth * (1.0 / (2 * SMOOTH + 1)) + FLOOR)
        inverse = inverse.reshape(channels, span, bins)
        for channel in range(channels):
            for k in range(2):
                white = values[channel, k] * inverse[channel]
                at = pl.ds(chunk * part + k * channels + channel, span, stride=2 * channels)
                for tile in range(bins // 128):
                    whole[tile, at, :] = white[:, tile * 128 : (tile + 1) * 128]
        at = pl.ds(chunk * part, part)
        for tile in range(bins // 128):
            mine[at, tile * 128 : (tile + 1) * 128] = whole[tile, at].astype(jnp.bfloat16)

    load_spectra.wait()
    for chunk in range(CHUNKS):
        whiten_part(chunk)
        if chunk == 0:
            neighbours = 3 + jnp.where(z > 0, 1, 0) + jnp.where(z < NZ - 1, 1, 0)
            pl.semaphore_wait(barrier, neighbours)
        to_mate(chunk).start()
    load_partners.wait()
    other = partners_ref[0, me] % 2 == 1
    for chunk in range(CHUNKS):
        to_mate(chunk).wait_recv()
        piece = pl.ds(chunk * part, part)
        gathered[me, piece] = jnp.where(other, mate[piece], mine[piece])
        for zc in range(NZ):
            pl.when(z == zc)(functools.partial(pass_on, zc, OWN, zc, chunk))

    @pl.loop(0, segments)
    def _(segment):
        block = mine[pl.ds(pl.multiple_of(segment * 2 * channels, 16), 2 * channels)]
        block = block.astype(jnp.float32)
        both = block[:channels] + block[channels:]
        for i in range(channels):
            rows_of = (block[i : i + 1], block[channels + i : channels + i + 1], both[i : i + 1])
            for place, row in enumerate(rows_of):
                bright[segment, i * 3 + place] = jnp.broadcast_to(row, (8, bins))

    load_table.wait()
    steps = plan()
    factor = math.sqrt(2.0 / (bins * segments))

    def take(zc, pieces):
        for column, plane, chunk in pieces:
            copy("x", column, plane, chunk).wait_recv()
            pass_on(zc, column, plane, chunk)

    packed = 0
    for zc in range(NZ):
        number = sum(code * 8**index for index, (code, _) in enumerate(steps[zc]))
        packed = jnp.where(z == zc, number, packed)

    def step(index, half, packed):
        code = packed % 8
        plane, dy = code // 2, code % 2
        pair = plane * 2 + y + dy - 2 * y * dy

        for tile in range(TILES):
            for zc in range(NZ):
                @pl.when(z == zc)
                def _():
                    for number, (_, pieces) in enumerate(steps[zc]):
                        if number % 2 == half and pieces[tile]:
                            pl.when(index == number)(functools.partial(take, zc, pieces[tile]))

            lanes = pl.ds(tile * 128, 128)

            for low in range(0, channels, channels // 2):
                own = range(low, low + channels // 2)

                def add(segment, sums):
                    sums = list(sums)
                    at = pl.ds(pl.multiple_of(segment * 2 * channels, 16), 2 * channels)
                    theirs = []
                    for side in range(2):
                        block = gathered[pair * 2 + side, at, lanes].astype(jnp.float32)
                        real, imag = block[:channels], block[channels:]
                        theirs.append((real, imag, real - imag))
                    place = 0
                    for i in own:
                        ours = [bright[segment, i * 3 + k, :, lanes] for k in range(3)]
                        for their in theirs:
                            for k in range(3):
                                sums[place] += ours[k] * their[k]
                                place += 1
                    return tuple(sums)

                zeros = tuple(jnp.zeros((8, 128), jnp.float32) for _ in range(3 * channels))
                sums = lax.fori_loop(0, segments, add, zeros, unroll=4)
                for number, i in enumerate(own):
                    left, right = sums[number * 6 : number * 6 + 3], sums[number * 6 + 3 : number * 6 + 6]
                    real = [part[0] + part[1] for part in (left, right)]
                    imag = [part[2] - part[0] + part[1] for part in (left, right)]
                    for o, both in enumerate((real, imag)):
                        at = pl.ds(tile * 128 + o * bins, 128)
                        cross[half, i * 16 : (i + 1) * 16, at] = jnp.concatenate(both, 0).astype(jnp.bfloat16)

        return pair

    def two_steps(index, packed):
        pairs = [step(index * 2 + half, half, packed // 8**half) for half in range(2)]
        table = table_ref[...].reshape(2 * bins, -1)
        left = cross[...].reshape(2 * channels * 16, 2 * bins)
        result = jnp.dot(left, table, preferred_element_type=jnp.float32)
        result = (result * factor).astype(jnp.bfloat16)
        for half, pair in enumerate(pairs):
            for i in range(channels):
                row = (half * channels + i) * 16
                held[pair, i] = result[row : row + 16, :lags]
            to_out(pair).start()
        return packed // 64

    def to_out(pair):
        at = pl.ds(pl.multiple_of(pair * 16, 16), 16)
        return pltpu.make_async_copy(held.at[pair], out_ref.at[:, 0, at], out_sem.at[pair])

    lax.fori_loop(0, NZ, two_steps, packed)
    for pair in range(2 * NZ):
        to_out(pair).wait()

    for chunk in range(CHUNKS):
        to_mate(chunk).wait_send()

    def drain(zc):
        pieces = [(OWN, zc, chunk) for chunk in range(CHUNKS)]
        pieces += [piece for _, tiles in steps[zc] for taken in tiles for piece in taken]
        for piece in pieces:
            for link in forwards(zc, *piece):
                copy(link, *piece).wait_send()

    for zc in range(NZ):
        pl.when(z == zc)(functools.partial(drain, zc))


def on_slice(spectra, partners):
    channels, _, segments, bins = spectra.shape
    members = lax.axis_size("mem")
    rows = segments * 2 * channels
    lags = bins + 1
    wide = -(-lags // 128) * 128
    table = np.zeros((2 * bins, wide), jnp.bfloat16)
    table[:, :lags] = lag_table(bins).reshape(2 * bins, lags)
    hbm = pl.BlockSpec(memory_space=pl.ANY)
    return pl.pallas_call(
        slice_kernel,
        out_shape=jax.ShapeDtypeStruct((channels, 1, members * channels, lags), jnp.bfloat16),
        in_specs=[hbm, hbm, hbm],
        out_specs=hbm,
        scratch_shapes=[
            pltpu.SMEM(partners.shape, jnp.int32),
            pltpu.VMEM(spectra.shape, jnp.bfloat16),
            pltpu.VMEM((2 * bins // 8, 8, wide), jnp.bfloat16),
            pltpu.SemaphoreType.DMA((3,)),
            pltpu.VMEM((members // 2, channels, 16, lags), jnp.bfloat16),
            pltpu.SemaphoreType.DMA((members // 2,)),
            pltpu.VMEM((bins // 128, rows, 128), jnp.float32),
            pltpu.VMEM((segments, 3 * channels, 8, bins), jnp.float32),
            pltpu.VMEM((rows, bins), jnp.bfloat16),
            pltpu.VMEM((rows, bins), jnp.bfloat16),
            pltpu.VMEM((members, rows, bins), jnp.bfloat16),
            pltpu.VMEM((2, 16 * channels, 2 * bins), jnp.bfloat16),
            pltpu.SemaphoreType.DMA((4, members, CHUNKS)),
            pltpu.SemaphoreType.DMA((members, CHUNKS)),
            pltpu.SemaphoreType.DMA((CHUNKS,)),
            pltpu.SemaphoreType.DMA((CHUNKS,)),
        ],
        compiler_params=pltpu.CompilerParams(
            collective_id=0, has_side_effects=True, vmem_limit_bytes=60 * 2**20
        ),
        cost_estimate=pl.CostEstimate(
            flops=2 * channels * members * channels * 2 * bins * lags,
            bytes_accessed=4 * 2**20,
            transcendentals=0,
        ),
    )(partners, spectra, jnp.asarray(table.reshape(-1, 8, wide)))


def solution(mesh):
    shape = (mesh.shape["grp"], mesh.shape["mem"])

    def on_device(spectra, partners):
        fits = spectra.shape == (8, 2, 16, 512) and partners.shape[0] == 1
        if shape == (2, 4 * NZ) and fits:
            return on_slice(spectra, partners)
        return any_mesh(spectra, partners)

    return jax.shard_map(
        on_device,
        mesh=mesh,
        in_specs=(P(("grp", "mem"), None, None, None), P()),
        out_specs=P(("grp", "mem"), None, None, None),
        check_vma=False,
    )
```
